32 devices in a mesh: fsdp: 16 (over z, y, x), ctx: 2 (over core).
Axes of the slice: x: 2, y: 2, z: 4, core: 2. Of those that a mesh axis runs over, the one named last changes fastest.
Arguments:
- hidden_states: bfloat16 [16, 768, 4096], P('fsdp', 'ctx'), may hold values from -20.4 to 20.4
- qkv_weight: bfloat16 [4096, 768], P('fsdp'), may hold values from -0.09375 to 0.09375
- doc_ids: int32 [16, 768], P('fsdp', 'ctx'), may hold values from 0 to 1, never falling along the last dimension, each value on 1 to 576 neighbouring positions
Outputs:
- context: bfloat16 [16, 768, 512], P('fsdp', 'ctx')
The draws below stay inside these ranges and needn't reach their ends.
Inputs may be any that keep to these rules, and one draw needn't show every extreme that they name: `doc_ids`: each sequence holds two documents one after the other, numbered 0 then 1, never falling; the first has 192 to 576 tokens and the second the rest.
All inputs are finite; a program needn't handle non-finite values.
Results may differ from the reference program's by a relative error of at most 0.012.
The reference program's roundings to bfloat16 on the way (of `queries`, `keys`, `values` and `probs`) count: a program that leaves them out, or rounds other values in their place, can miss the bound.
Values may be sent and summed in bfloat16 or wider, within the bound.
No kernel may reach another device: no remote copies, remote signals or barrier semaphores. Data moves between devices by JAX's collectives and lax.ppermute only.
A program may use at most 64 MiB of HBM per device.

```python
import math
import jax
import jax.numpy as jnp
import numpy as np
from jax import lax

D = 4096
HEADS = 4
HD = 128
TOK_DEV = 384
SEQ = 768
SEQS = 16
COLS = 768


def draw_hidden_states(key, part):
    key_one = jax.random.fold_in(jax.random.fold_in(key, 11), 0)
    bulk_values = jax.random.normal(key_one, (SEQS, SEQ, D), jnp.float32)
    return jnp.clip(bulk_values, -6.0, 6.0).astype(jnp.bfloat16)


def levels(key, shape, cuts, low, high):
    factor_of = 1.0
    for dim, parts in cuts:
        draws = jax.random.uniform(jax.random.fold_in(jax.random.fold_in(key, 6), dim), (parts,), jnp.float32, low / len(cuts), high / len(cuts))
        factor_of = factor_of * jnp.repeat(jnp.exp(draws), shape[dim] // parts).reshape((-1,) + (1,) * (len(shape) - 1 - dim))
    return factor_of


def length_profile(amount, total, limit, lean):
    weights = [(1 << 20) // math.isqrt(rank ** lean) + 1 for rank in range(2, amount + 1)]
    spare, given = total - limit - (amount - 1), [1] * (amount - 1)
    while spare > 0:
        free = [i for i in range(amount - 1) if given[i] < limit]
        pool, remaining = sum([weights[i] for i in free]), spare
        for i in free:
            extra = min(limit - given[i], max(1, remaining * weights[i] // pool), spare)
            given[i] = given[i] + extra
            spare = spare - extra
    return np.array([limit] + given)


def uneven_parts(rng, number_of, total, limit, slope):
    if number_of == 2:
        one = jax.random.randint(rng, (), max(1, total - limit), min(limit, total - 1) + 1)
        return jnp.stack([one, total - one])
    sizes = jnp.asarray(length_profile(number_of, total, limit, slope), jnp.int32)
    pairs = (number_of - 1) // 2
    giver, receiver = sizes[1:1 + 2 * pairs:2], sizes[2:2 + 2 * pairs:2]
    room = jnp.minimum(giver - 1, limit - receiver)
    shifted = jax.random.randint(jax.random.fold_in(rng, 1), (pairs,), 0, 1 << 20) % (room + 1)
    sizes = sizes.at[1:1 + 2 * pairs:2].set(giver - shifted).at[2:2 + 2 * pairs:2].set(receiver + shifted)
    return sizes[jax.random.permutation(jax.random.fold_in(rng, 2), number_of)]


def gaussian(rng, dims, scale, limit, cuts=(), held_as=jnp.bfloat16):
    loudness = levels(rng, dims, cuts, -0.22, 0.18) if cuts else 1.0
    array = jax.random.normal(rng, dims, jnp.float32) * scale * loudness
    return jnp.minimum(jnp.maximum(array, -limit), limit).astype(held_as)


def setup_inputs(seed: int = 0) -> dict:
    arg_keys = jax.random.split(jax.random.key(seed), 4)
    hidden_states = draw_hidden_states(jax.random.fold_in(arg_keys[3], 71), 0)
    qkv_weight = gaussian(arg_keys[1], (D, COLS), D ** -0.5, 0.09375, ((0, 16),))
    doc_ids = jax.vmap(lambda own: jnp.searchsorted(jnp.cumsum(uneven_parts(own, 2, SEQ, SEQ - TOK_DEV // 2, 0)), jnp.arange(SEQ), side="right"))(jax.random.split(arg_keys[2], SEQS)).reshape((SEQS, SEQ)).astype(jnp.int32)
    return dict(hidden_states=hidden_states, qkv_weight=qkv_weight, doc_ids=doc_ids)


THETA = 1000000.0

def rotary(values_in, positions):
    half_width = values_in.shape[-1] // 2
    frequency = jnp.exp(jnp.arange(half_width, dtype=jnp.float32) * (-2.0 * math.log(THETA) / values_in.shape[-1]))
    angles = positions * frequency
    cosine = jnp.cos(angles)
    sine_part = jnp.sin(angles)
    lower_half = values_in[..., :half_width]
    upper_half = values_in[..., half_width:]
    return jnp.concatenate([lower_half * cosine - upper_half * sine_part, upper_half * cosine + lower_half * sine_part], axis=-1)

def reference(hidden_states, qkv_weight, doc_ids):
    scale = 1.0 / math.sqrt(HD)

    def one_sequence(inputs):
        tokens, documents = inputs
        length = tokens.shape[0]
        projected = jnp.dot(tokens, qkv_weight, preferred_element_type=jnp.float32)
        positions = jnp.arange(length, dtype=jnp.int32).astype(jnp.float32)
        queries = rotary(projected[:, :HEADS * HD].reshape(length, HEADS, HD), positions[:, None, None]).astype(jnp.bfloat16)
        keys = rotary(projected[:, HEADS * HD:(HEADS + 1) * HD], positions[:, None]).astype(jnp.bfloat16)
        values = projected[:, (HEADS + 1) * HD:].astype(jnp.bfloat16)
        scores = jnp.einsum('qhd,kd->hqk', queries.astype(jnp.float32), keys.astype(jnp.float32)) * scale
        index = jnp.arange(length, dtype=jnp.int32)
        visible = (index[None, :] <= index[:, None]) & (documents[None, :] == documents[:, None])
        scores = jnp.where(visible[None], scores, -jnp.inf)
        row_max = lax.optimization_barrier(jnp.max(scores, axis=-1, keepdims=True))
        weights = jnp.exp(scores - row_max)
        totals = lax.optimization_barrier(jnp.sum(weights, axis=-1))
        probs = weights.astype(jnp.bfloat16)
        summed = jnp.einsum('hqk,kd->hqd', probs.astype(jnp.float32), values.astype(jnp.float32))
        context = (summed / totals[..., None]).astype(jnp.bfloat16)
        return jnp.transpose(context, (1, 0, 2)).reshape(length, HEADS * HD)
    return lax.map(one_sequence, (hidden_states, doc_ids))
```

```python
import functools
import math

import jax
import jax.numpy as jnp
from jax import lax
from jax.experimental import pallas as pl
from jax.experimental.pallas import tpu as pltpu
from jax.sharding import PartitionSpec as P

HEADS = 4
HD = 128


THETA = 1000000.0

VMEM_LIMIT = 40 * 1024 * 1024


def shifted(value, axis, steps):
    count = lax.axis_size(axis)
    first, last = (max(0, -steps), min(count, count - steps))
    return lax.ppermute(value, axis, [(source, source + steps) for source in range(first, last)])


def rotary(values_in, positions):
    half_width = values_in.shape[-1] // 2
    frequency = jnp.exp(
        jnp.arange(half_width, dtype=jnp.float32) * (-2.0 * math.log(THETA) / values_in.shape[-1])
    )
    angles = positions * frequency
    cosine = jnp.cos(angles)
    sine_part = jnp.sin(angles)
    lower_half = values_in[..., :half_width]
    upper_half = values_in[..., half_width:]
    return jnp.concatenate(
        [
            lower_half * cosine - upper_half * sine_part,
            upper_half * cosine + lower_half * sine_part,
        ],
        axis=-1,
    )


def ring_body(hidden_states, qkv_weight, doc_ids):
    tokens = hidden_states[0]
    row_count = tokens.shape[0]
    projected = jnp.dot(
        tokens,
        lax.all_gather(qkv_weight, "fsdp", axis=0, tiled=True),
        preferred_element_type=jnp.float32,
    )
    ctx_count = lax.axis_size("ctx")
    ctx_index = lax.axis_index("ctx")
    row_start = ctx_index * row_count
    local_index = jnp.arange(row_count, dtype=jnp.int32)
    query_pos = row_start + local_index
    positions = query_pos.astype(jnp.float32)
    queries = rotary(
        projected[:, : HEADS * HD].reshape(row_count, HEADS, HD), positions[:, None, None]
    ).astype(jnp.bfloat16)
    keys_here = rotary(projected[:, HEADS * HD : (HEADS + 1) * HD], positions[:, None]).astype(
        jnp.bfloat16
    )
    values_here = projected[:, (HEADS + 1) * HD :].astype(jnp.bfloat16)
    docs_wire = doc_ids[0]
    scale = 1.0 / math.sqrt(HD)

    def attend(state, key_block, value_block, doc_block, key_first):
        running_max, running_sum, running_acc = state
        scores = (
            jnp.einsum("qhd,kd->hqk", queries, key_block, preferred_element_type=jnp.float32)
            * scale
        )
        key_pos = key_first + jnp.arange(key_block.shape[0], dtype=jnp.int32)
        visible = (key_pos[None, :] <= query_pos[:, None]) & (
            doc_block[None, :] == docs_wire[:, None]
        )
        scores = jnp.where(visible[None], scores, -jnp.inf)
        new_max = jnp.maximum(running_max, jnp.max(scores, axis=-1))
        weights = jnp.exp(scores - new_max[..., None])
        factor = jnp.exp(running_max - new_max)
        new_sum = running_sum * factor + jnp.sum(weights, axis=-1)
        update = jnp.einsum(
            "hqk,kd->hqd",
            weights.astype(jnp.bfloat16),
            value_block,
            preferred_element_type=jnp.float32,
        )
        new_acc = running_acc * factor[..., None] + update
        return (new_max, new_sum, new_acc)

    state = (
        jnp.full((HEADS, row_count), -jnp.inf, jnp.float32),
        jnp.zeros((HEADS, row_count), jnp.float32),
        jnp.zeros((HEADS, row_count, HD), jnp.float32),
    )
    state = attend(state, keys_here, values_here, docs_wire, row_start)
    travelling = (keys_here, values_here, docs_wire)
    for rotation in range(1, ctx_count):
        travelling = shifted((travelling[0], travelling[1], travelling[2]), "ctx", 1)
        key_first = (ctx_index - rotation) * row_count
        arrived = travelling

        def take_block(current):
            return attend(current, arrived[0], arrived[1], arrived[2], key_first)

        def keep_block(current):
            return current

        state = lax.cond(rotation <= ctx_index, take_block, keep_block, state)
    context = state[2] / state[1][..., None]
    context = jnp.transpose(context.astype(jnp.bfloat16), (1, 0, 2)).reshape(row_count, HEADS * HD)
    return context[None]


def flip(value, first_mask, second_mask):
    count = lax.axis_size("fsdp")
    pairs = []
    for chip in range(count):
        pairs.append((chip * 2, (chip ^ first_mask) * 2))
        pairs.append((chip * 2 + 1, (chip ^ second_mask) * 2 + 1))
    return lax.ppermute(value, ("fsdp", "ctx"), pairs)


def swap(value):
    return lax.ppermute(value, "ctx", [(0, 1), (1, 0)])


def after(value, *others):
    return lax.optimization_barrier((value,) + others)[0]


def add_blocks(total, parts, masks, mine_ref, other_ref, held, sems):
    rows = parts[0].shape[0]
    chip = lax.axis_index("fsdp")
    core = lax.axis_index("ctx")
    copies = []
    for place, (first_mask, second_mask) in enumerate(masks):
        source = jnp.where(core == 0, chip ^ first_mask, chip ^ second_mask)
        columns = pl.ds(pl.multiple_of(source * rows, rows), rows)
        for side, ref in enumerate((mine_ref, other_ref)):
            copy = pltpu.make_async_copy(
                ref.at[:, columns], held.at[side, place], sems.at[side, place]
            )
            copy.start()
            copies.append(copy)
    sums = [None, None] if total is None else [total[0], total[1]]
    for place, part in enumerate(parts):
        weights = part[...]
        for side in range(2):
            copies[place * 2 + side].wait()
            term = jnp.dot(held[side, place], weights, preferred_element_type=jnp.float32)
            sums[side] = term if sums[side] is None else sums[side] + term
    return sums


def partial_kernel(masks, begun, *refs):
    count = len(masks)
    mine_ref, other_ref = refs[:2]
    parts = refs[2 : 2 + count]
    rest = refs[2 + count :]
    total = None
    if begun:
        total, rest = rest[0], rest[1:]
    out_ref, held, sems = rest
    sums = add_blocks(total, parts, masks, mine_ref, other_ref, held, sems)
    out_ref[0] = sums[0]
    out_ref[1] = sums[1]


def final_kernel(masks, *refs):
    count = len(masks)
    mine_ref, other_ref = refs[:2]
    parts = refs[2 : 2 + count]
    total, cos_ref, sin_ref, keep_ref, send_ref, held, sems = refs[2 + count :]
    sums = add_blocks(total, parts, masks, mine_ref, other_ref, held, sems)
    turned = lax.axis_index("ctx") == 0

    def turn(block, cosine, sine):
        swapped = jnp.concatenate([block[:, HD // 2 :], block[:, : HD // 2]], axis=1)
        return (block * cosine + swapped * sine).astype(jnp.bfloat16)

    ends = []
    for side in range(2):
        cosine, sine = cos_ref[side], sin_ref[side]
        blocks = [
            turn(sums[side][:, :HD], cosine, sine),
            turn(sums[side][:, HD : 2 * HD], cosine, sine),
            turn(
                sums[side][:, 2 * HD :],
                jnp.where(turned, cosine, 1.0),
                jnp.where(turned, sine, 0.0),
            ),
        ]
        ends.append(blocks)
    for ref, here, there in ((keep_ref, ends[0], ends[1]), (send_ref, ends[1], ends[0])):
        ref[:, :HD] = here[0]
        ref[:, HD : 2 * HD] = here[1]
        ref[:, 2 * HD : 3 * HD] = here[2]
        ref[:, 3 * HD :] = there[2]


def attention_kernel(keep_ref, recv_ref, docs_q_ref, docs_k_ref, out_ref):
    core = lax.axis_index("ctx")
    rows = keep_ref.shape[0]
    tile = 128
    kept = jnp.concatenate([keep_ref[:, 3 * HD :], keep_ref[:, 2 * HD : 3 * HD]], axis=0)
    received = jnp.concatenate([recv_ref[:, 3 * HD :], recv_ref[:, 2 * HD : 3 * HD]], axis=0)
    keys = jnp.where(core == 0, kept, received)
    values = jnp.where(core == 0, received, kept)
    factor = math.log2(math.e) / math.sqrt(HD)
    kept_first = pl.multiple_of(core * 2 * HD, 2 * HD)
    recv_first = pl.multiple_of((1 - core) * 2 * HD, 2 * HD)
    for step in range(rows // tile):
        here = slice(step * tile, (step + 1) * tile)
        width = rows + (step + 1) * tile
        queries = jnp.concatenate(
            [
                keep_ref[here, :HD],
                keep_ref[here, HD : 2 * HD],
                recv_ref[here, :HD],
                recv_ref[here, HD : 2 * HD],
            ],
            axis=0,
        )
        scores = lax.dot_general(
            queries, keys[:width], (((1,), (1,)), ((), ())), preferred_element_type=jnp.float32
        )
        column = lax.broadcasted_iota(jnp.int32, (tile, width), 1)
        row = lax.broadcasted_iota(jnp.int32, (tile, width), 0) + (rows + step * tile)
        first = jnp.where(core == 0, rows, 0)
        visible = (
            (column <= row) & (column >= first) & (docs_q_ref[here, :] == docs_k_ref[:, :width])
        )
        scores = jnp.where(visible[None], scores.reshape(HEADS, tile, width), -jnp.inf)
        top = jnp.max(scores, axis=-1, keepdims=True)
        weights = jnp.exp2((scores - top) * factor)
        totals = jnp.sum(weights, axis=-1, keepdims=True)
        context = jnp.dot(
            weights.astype(jnp.bfloat16).reshape(HEADS * tile, width),
            values[:width],
            preferred_element_type=jnp.float32,
        ).reshape(HEADS, tile, HD)
        context = (context / totals).astype(jnp.bfloat16)
        for head in range(HEADS // 2):
            out_ref[here, pl.ds(pl.multiple_of(kept_first + head * HD, HD), HD)] = context[head]
            out_ref[here, pl.ds(pl.multiple_of(recv_first + head * HD, HD), HD)] = context[
                head + HEADS // 2
            ]


VMEM = pl.BlockSpec(memory_space=pltpu.VMEM)
ANY = pl.BlockSpec(memory_space=pl.ANY)


def partial(mine, other, parts, masks, total=None, tables=None):
    rows, width = parts[0].shape
    tokens = mine.shape[0]
    count = len(parts)
    begun = total is not None
    scratch = [
        pltpu.VMEM((2, count, tokens, rows), mine.dtype),
        pltpu.SemaphoreType.DMA((2, count)),
    ]
    cost = pl.CostEstimate(
        flops=4 * tokens * rows * width * count,
        bytes_accessed=count * rows * (width + 2 * tokens) * 2 + 16 * tokens * width,
        transcendentals=0,
    )
    params = pltpu.CompilerParams(vmem_limit_bytes=VMEM_LIMIT)
    if tables is None:
        return pl.pallas_call(
            functools.partial(partial_kernel, masks, begun),
            out_shape=jax.ShapeDtypeStruct((2, tokens, width), jnp.float32),
            in_specs=[ANY, ANY] + [VMEM] * (count + begun),
            out_specs=VMEM,
            scratch_shapes=scratch,
            compiler_params=params,
            cost_estimate=cost,
        )(mine, other, *parts, *([total] if begun else []))
    out = jax.ShapeDtypeStruct((tokens, 4 * HD), jnp.bfloat16)
    return pl.pallas_call(
        functools.partial(final_kernel, masks),
        out_shape=(out, out),
        in_specs=[ANY, ANY] + [VMEM] * (count + 3),
        out_specs=(VMEM, VMEM),
        scratch_shapes=scratch,
        compiler_params=params,
        cost_estimate=cost,
    )(mine, other, *parts, total, *tables)


def paired_body(hidden_states, qkv_weight, doc_ids):
    mine = hidden_states[0]
    tokens = mine.shape[0]
    core = lax.axis_index("ctx")
    own = jnp.concatenate(
        [
            lax.dynamic_slice_in_dim(qkv_weight, core * 2 * HD, 2 * HD, 1),
            lax.dynamic_slice_in_dim(qkv_weight, (HEADS + core) * HD, HD, 1),
        ],
        axis=1,
    )

    near = flip(own, 4, 4)
    slots = [(own, 0), (near, 4), (flip(own, 8, 8), 8), (flip(after(own, near), 12, 12), 12)]
    parts, masks = [], []
    for block, base in slots:
        one = flip(block, 1, 2)
        two = flip(block, 2, 1)
        both = flip(one, 2, 1)
        parts += [block, one, two, both]
        masks += [(base, base), (base ^ 1, base ^ 2), (base ^ 2, base ^ 1), (base ^ 3, base ^ 3)]

    other = swap(mine)
    docs_other = swap(doc_ids)
    docs_q = doc_ids.reshape(tokens, 1)
    docs_k = jnp.concatenate([docs_other, doc_ids], axis=1)

    frequency = jnp.exp(
        jnp.arange(HD // 2, dtype=jnp.float32) * (-2.0 * math.log(THETA) / HD)
    )
    starts = jnp.stack([core, 1 - core])[:, None] * tokens
    positions = (starts + jnp.arange(tokens, dtype=jnp.int32)[None]).astype(jnp.float32)
    angles = positions[..., None] * frequency
    cosine, sine = jnp.cos(angles), jnp.sin(angles)
    cosines = jnp.concatenate([cosine, cosine], axis=-1)
    sines = jnp.concatenate([-sine, sine], axis=-1)

    mine_in, cosines, sines, docs_q, docs_k = lax.optimization_barrier(
        (mine, cosines, sines, docs_q, docs_k)
    )
    total = partial(mine_in, other, parts[:8], masks[:8])
    total = partial(mine_in, other, parts[8:15], masks[8:15], total)
    keep, send = partial(mine_in, other, parts[15:], masks[15:], total, (cosines, sines))
    recv = swap(send)
    context = pl.pallas_call(
        attention_kernel,
        out_shape=jax.ShapeDtypeStruct((tokens, HEADS * HD), jnp.bfloat16),
        in_specs=[VMEM] * 4,
        out_specs=VMEM,
        compiler_params=pltpu.CompilerParams(vmem_limit_bytes=VMEM_LIMIT),
        cost_estimate=pl.CostEstimate(
            flops=8 * HEADS * tokens * tokens * HD,
            bytes_accessed=tokens * HD * 32,
            transcendentals=2 * HEADS * tokens * tokens,
        ),
    )(keep, recv, docs_q, docs_k)
    return context[None]


def solution(mesh):
    in_specs = (P("fsdp", "ctx", None), P("fsdp", None), P("fsdp", "ctx"))
    out_specs = P("fsdp", "ctx", None)
    paired = mesh.shape["fsdp"] == 16 and mesh.shape["ctx"] == 2
    body = paired_body if paired else ring_body
    return jax.shard_map(body, mesh=mesh, in_specs=in_specs, out_specs=out_specs, check_vma=False)
```

```python
import functools
import math

import jax
import jax.numpy as jnp
from jax import lax
from jax.experimental import pallas as pl
from jax.experimental.pallas import tpu as pltpu
from jax.sharding import PartitionSpec as P

HEADS = 4
HD = 128


THETA = 1000000.0

TILE = 16

VMEM_LIMIT = 16 * 1024 * 1024


def shifted(value, axis, steps):
    count = lax.axis_size(axis)
    first, last = (max(0, -steps), min(count, count - steps))
    return lax.ppermute(value, axis, [(source, source + steps) for source in range(first, last)])


def rotary(values_in, positions):
    half_width = values_in.shape[-1] // 2
    frequency = jnp.exp(
        jnp.arange(half_width, dtype=jnp.float32) * (-2.0 * math.log(THETA) / values_in.shape[-1])
    )
    angles = positions * frequency
    cosine = jnp.cos(angles)
    sine_part = jnp.sin(angles)
    lower_half = values_in[..., :half_width]
    upper_half = values_in[..., half_width:]
    return jnp.concatenate(
        [
            lower_half * cosine - upper_half * sine_part,
            upper_half * cosine + lower_half * sine_part,
        ],
        axis=-1,
    )


def ring_body(hidden_states, qkv_weight, doc_ids):
    tokens = hidden_states[0]
    row_count = tokens.shape[0]
    projected = jnp.dot(
        tokens,
        lax.all_gather(qkv_weight, "fsdp", axis=0, tiled=True),
        preferred_element_type=jnp.float32,
    )
    ctx_count = lax.axis_size("ctx")
    ctx_index = lax.axis_index("ctx")
    row_start = ctx_index * row_count
    local_index = jnp.arange(row_count, dtype=jnp.int32)
    query_pos = row_start + local_index
    positions = query_pos.astype(jnp.float32)
    queries = rotary(
        projected[:, : HEADS * HD].reshape(row_count, HEADS, HD), positions[:, None, None]
    ).astype(jnp.bfloat16)
    keys_here = rotary(projected[:, HEADS * HD : (HEADS + 1) * HD], positions[:, None]).astype(
        jnp.bfloat16
    )
    values_here = projected[:, (HEADS + 1) * HD :].astype(jnp.bfloat16)
    docs_wire = doc_ids[0]
    scale = 1.0 / math.sqrt(HD)

    def attend(state, key_block, value_block, doc_block, key_first):
        running_max, running_sum, running_acc = state
        scores = (
            jnp.einsum("qhd,kd->hqk", queries, key_block, preferred_element_type=jnp.float32)
            * scale
        )
        key_pos = key_first + jnp.arange(key_block.shape[0], dtype=jnp.int32)
        visible = (key_pos[None, :] <= query_pos[:, None]) & (
            doc_block[None, :] == docs_wire[:, None]
        )
        scores = jnp.where(visible[None], scores, -jnp.inf)
        new_max = jnp.maximum(running_max, jnp.max(scores, axis=-1))
        weights = jnp.exp(scores - new_max[..., None])
        factor = jnp.exp(running_max - new_max)
        new_sum = running_sum * factor + jnp.sum(weights, axis=-1)
        update = jnp.einsum(
            "hqk,kd->hqd",
            weights.astype(jnp.bfloat16),
            value_block,
            preferred_element_type=jnp.float32,
        )
        new_acc = running_acc * factor[..., None] + update
        return (new_max, new_sum, new_acc)

    state = (
        jnp.full((HEADS, row_count), -jnp.inf, jnp.float32),
        jnp.zeros((HEADS, row_count), jnp.float32),
        jnp.zeros((HEADS, row_count, HD), jnp.float32),
    )
    state = attend(state, keys_here, values_here, docs_wire, row_start)
    travelling = (keys_here, values_here, docs_wire)
    for rotation in range(1, ctx_count):
        travelling = shifted((travelling[0], travelling[1], travelling[2]), "ctx", 1)
        key_first = (ctx_index - rotation) * row_count
        arrived = travelling

        def take_block(current):
            return attend(current, arrived[0], arrived[1], arrived[2], key_first)

        def keep_block(current):
            return current

        state = lax.cond(rotation <= ctx_index, take_block, keep_block, state)
    context = state[2] / state[1][..., None]
    context = jnp.transpose(context.astype(jnp.bfloat16), (1, 0, 2)).reshape(row_count, HEADS * HD)
    return context[None]


def flip(value, first_mask, second_mask):
    count = lax.axis_size("fsdp")
    pairs = []
    for chip in range(count):
        pairs.append((chip * 2, (chip ^ first_mask) * 2))
        pairs.append((chip * 2 + 1, (chip ^ second_mask) * 2 + 1))
    return lax.ppermute(value, ("fsdp", "ctx"), pairs)


def swap(value):
    return lax.ppermute(value, "ctx", [(0, 1), (1, 0)])


def after(value, *others):
    return lax.optimization_barrier((value,) + others)[0]


def add_blocks(total, parts, masks, mine_ref, other_ref):
    rows = parts[0].shape[0]
    chip = lax.axis_index("fsdp")
    core = lax.axis_index("ctx")
    sums = [None, None] if total is None else [total[0], total[1]]
    for part, (first_mask, second_mask) in zip(parts, masks):
        source = jnp.where(core == 0, chip ^ first_mask, chip ^ second_mask)
        columns = pl.ds(pl.multiple_of(source * rows, rows), rows)
        weights = part[...]
        for side, ref in enumerate((mine_ref, other_ref)):
            term = jnp.dot(ref[:, columns], weights, preferred_element_type=jnp.float32)
            sums[side] = term if sums[side] is None else sums[side] + term
    return sums


def partial_kernel(masks, begun, *refs):
    count = len(masks)
    mine_ref, other_ref = refs[:2]
    parts = refs[2 : 2 + count]
    rest = refs[2 + count :]
    total = None
    if begun:
        total, rest = rest[0], rest[1:]
    (out_ref,) = rest
    sums = add_blocks(total, parts, masks, mine_ref, other_ref)
    out_ref[0] = sums[0]
    out_ref[1] = sums[1]


def final_kernel(masks, *refs):
    count = len(masks)
    mine_ref, other_ref = refs[:2]
    parts = refs[2 : 2 + count]
    total, cos_ref, sin_ref, docs_ref, keep_ref, send_ref = refs[2 + count :]
    sums = add_blocks(total, parts, masks, mine_ref, other_ref)
    turned = lax.axis_index("ctx") == 0

    def turn(block, cosine, sine):
        swapped = jnp.concatenate([block[:, HD // 2 :], block[:, : HD // 2]], axis=1)
        return (block * cosine + swapped * sine).astype(jnp.bfloat16)

    ends = []
    for side in range(2):
        cosine, sine = cos_ref[side], sin_ref[side]
        blocks = [
            turn(sums[side][:, :HD], cosine, sine),
            turn(sums[side][:, HD : 2 * HD], cosine, sine),
            turn(
                sums[side][:, 2 * HD :],
                jnp.where(turned, cosine, 1.0),
                jnp.where(turned, sine, 0.0),
            ),
        ]
        ends.append(blocks)
    rows = docs_ref.shape[1]
    for ref, here, there in ((keep_ref, ends[0], ends[1]), (send_ref, ends[1], ends[0])):
        ref[:rows, :HD] = here[0]
        ref[:rows, HD : 2 * HD] = here[1]
        ref[:rows, 2 * HD : 3 * HD] = here[2]
        ref[:rows, 3 * HD :] = there[2]
        ref[rows:, :] = jnp.zeros((TILE, 4 * HD), ref.dtype)
        ref[rows:, :rows] = jnp.broadcast_to(docs_ref[...], (TILE, rows)).astype(ref.dtype)


def attention_kernel(keep_ref, recv_ref, docs_ref, out_ref):
    core = lax.axis_index("ctx")
    rows = docs_ref.shape[0]
    tile = 128
    kept = jnp.concatenate([keep_ref[:rows, 3 * HD :], keep_ref[:rows, 2 * HD : 3 * HD]], axis=0)
    received = jnp.concatenate([recv_ref[:rows, 3 * HD :], recv_ref[:rows, 2 * HD : 3 * HD]], axis=0)
    keys = jnp.where(core == 0, kept, received)
    values = jnp.where(core == 0, received, kept)
    docs = jnp.concatenate(
        [recv_ref[rows : rows + 1, :rows], keep_ref[rows : rows + 1, :rows]], axis=1
    ).astype(jnp.float32)
    factor = math.log2(math.e) / math.sqrt(HD)
    kept_first = pl.multiple_of(core * 2 * HD, 2 * HD)
    recv_first = pl.multiple_of((1 - core) * 2 * HD, 2 * HD)
    for step in range(rows // tile):
        here = slice(step * tile, (step + 1) * tile)
        width = rows + (step + 1) * tile
        queries = jnp.concatenate(
            [
                keep_ref[here, :HD],
                keep_ref[here, HD : 2 * HD],
                recv_ref[here, :HD],
                recv_ref[here, HD : 2 * HD],
            ],
            axis=0,
        )
        scores = lax.dot_general(
            queries, keys[:width], (((1,), (1,)), ((), ())), preferred_element_type=jnp.float32
        )
        column = lax.broadcasted_iota(jnp.int32, (tile, width), 1)
        row = lax.broadcasted_iota(jnp.int32, (tile, width), 0) + (rows + step * tile)
        first = jnp.where(core == 0, rows, 0)
        visible = (
            (column <= row) & (column >= first) & (docs_ref[here, :] == docs[:, :width])
        )
        scores = jnp.where(visible[None], scores.reshape(HEADS, tile, width), -jnp.inf)
        top = jnp.max(scores, axis=-1, keepdims=True)
        weights = jnp.exp2((scores - top) * factor)
        totals = jnp.sum(weights, axis=-1, keepdims=True)
        context = jnp.dot(
            weights.astype(jnp.bfloat16).reshape(HEADS * tile, width),
            values[:width],
            preferred_element_type=jnp.float32,
        ).reshape(HEADS, tile, HD)
        context = (context / totals).astype(jnp.bfloat16)
        for head in range(HEADS // 2):
            out_ref[here, pl.ds(pl.multiple_of(kept_first + head * HD, HD), HD)] = context[head]
            out_ref[here, pl.ds(pl.multiple_of(recv_first + head * HD, HD), HD)] = context[
                head + HEADS // 2
            ]


VMEM = pl.BlockSpec(memory_space=pltpu.VMEM)


def stage_kernel(source_ref, out_ref, sem):
    copy = pltpu.make_async_copy(source_ref, out_ref, sem)
    copy.start()
    copy.wait()


def stage(value):
    return pl.pallas_call(
        stage_kernel,
        out_shape=jax.ShapeDtypeStruct(value.shape, value.dtype),
        in_specs=[pl.BlockSpec(memory_space=pl.ANY)],
        out_specs=VMEM,
        scratch_shapes=[pltpu.SemaphoreType.DMA],
        compiler_params=pltpu.CompilerParams(vmem_limit_bytes=VMEM_LIMIT),
        cost_estimate=pl.CostEstimate(flops=0, bytes_accessed=2 * value.size * 2, transcendentals=0),
    )(value)


def partial(mine, other, parts, masks, total=None, tables=None):
    rows, width = parts[0].shape
    tokens = mine.shape[0]
    count = len(parts)
    begun = total is not None
    cost = pl.CostEstimate(
        flops=4 * tokens * rows * width * count,
        bytes_accessed=count * rows * (width + 2 * tokens) * 2 + 16 * tokens * width,
        transcendentals=0,
    )
    params = pltpu.CompilerParams(vmem_limit_bytes=VMEM_LIMIT)
    if tables is None:
        return pl.pallas_call(
            functools.partial(partial_kernel, masks, begun),
            out_shape=jax.ShapeDtypeStruct((2, tokens, width), jnp.float32),
            in_specs=[VMEM] * (2 + count + begun),
            out_specs=VMEM,
            compiler_params=params,
            cost_estimate=cost,
        )(mine, other, *parts, *([total] if begun else []))
    out = jax.ShapeDtypeStruct((tokens + TILE, 4 * HD), jnp.bfloat16)
    return pl.pallas_call(
        functools.partial(final_kernel, masks),
        out_shape=(out, out),
        in_specs=[VMEM] * (count + 6),
        out_specs=(VMEM, VMEM),
        compiler_params=params,
        cost_estimate=cost,
    )(mine, other, *parts, total, *tables)


def paired_body(hidden_states, qkv_weight, doc_ids):
    mine = hidden_states[0]
    tokens = mine.shape[0]
    core = lax.axis_index("ctx")
    own = jnp.concatenate(
        [
            lax.dynamic_slice_in_dim(qkv_weight, core * 2 * HD, 2 * HD, 1),
            lax.dynamic_slice_in_dim(qkv_weight, (HEADS + core) * HD, HD, 1),
        ],
        axis=1,
    )

    frequency = jnp.exp(
        jnp.arange(HD // 2, dtype=jnp.float32) * (-2.0 * math.log(THETA) / HD)
    )
    starts = jnp.stack([core, 1 - core])[:, None] * tokens
    positions = (starts + jnp.arange(tokens, dtype=jnp.int32)[None]).astype(jnp.float32)
    angles = positions[..., None] * frequency
    cosine, sine = jnp.cos(angles), jnp.sin(angles)
    cosines = jnp.concatenate([cosine, cosine], axis=-1)
    sines = jnp.concatenate([-sine, sine], axis=-1)
    docs = doc_ids.reshape(tokens, 1).astype(jnp.float32)

    z1 = flip(own, 4, 4)
    z2 = flip(own, 8, 8)
    a0 = flip(own, 1, 2)
    b0 = flip(own, 2, 1)
    z3 = flip(z2, 4, 4)

    other = stage(swap(mine))
    z1, cosines, sines, docs, other = lax.optimization_barrier(
        (z1, cosines, sines, docs, other)
    )
    a1, b1, c0 = flip(z1, 1, 2), flip(z1, 2, 1), flip(a0, 2, 1)
    a2, b2, c1 = flip(z2, 1, 2), flip(z2, 2, 1), flip(a1, 2, 1)
    a3, b3, c2 = flip(z3, 1, 2), flip(z3, 2, 1), flip(a2, 2, 1)
    total = partial(
        mine,
        other,
        [own, a0, b0, c0, z1, a1, b1, z2],
        [(0, 0), (1, 2), (2, 1), (3, 3), (4, 4), (5, 6), (6, 5), (8, 8)],
    )
    a3, total = lax.optimization_barrier((a3, total))
    c3 = flip(a3, 2, 1)
    total = partial(
        mine, other, [c1, a2, b2, z3], [(7, 7), (9, 10), (10, 9), (12, 12)], total
    )
    total = partial(mine, other, [c2, a3, b3], [(11, 11), (13, 14), (14, 13)], total)
    keep, send = partial(mine, other, [c3], [(15, 15)], total, (cosines, sines, doc_ids))
    recv = swap(send)
    context = pl.pallas_call(
        attention_kernel,
        out_shape=jax.ShapeDtypeStruct((tokens, HEADS * HD), jnp.bfloat16),
        in_specs=[VMEM] * 3,
        out_specs=VMEM,
        compiler_params=pltpu.CompilerParams(vmem_limit_bytes=VMEM_LIMIT),
        cost_estimate=pl.CostEstimate(
            flops=8 * HEADS * tokens * tokens * HD,
            bytes_accessed=tokens * HD * 32,
            transcendentals=2 * HEADS * tokens * tokens,
        ),
    )(keep, recv, docs)
    return context[None]


def solution(mesh):
    in_specs = (P("fsdp", "ctx", None), P("fsdp", None), P("fsdp", "ctx"))
    out_specs = P("fsdp", "ctx", None)
    paired = mesh.shape["fsdp"] == 16 and mesh.shape["ctx"] == 2
    body = paired_body if paired else ring_body
    return jax.shard_map(body, mesh=mesh, in_specs=in_specs, out_specs=out_specs, check_vma=False)
```

```python
import functools
import math

import jax
import jax.numpy as jnp
from jax import lax
from jax.experimental import pallas as pl
from jax.experimental.pallas import tpu as pltpu
from jax.sharding import PartitionSpec as P

HEADS = 4
HD = 128


THETA = 1000000.0

STEP = 128

VMEM_LIMIT = 16 * 1024 * 1024


def shifted(value, axis, steps):
    count = lax.axis_size(axis)
    first, last = (max(0, -steps), min(count, count - steps))
    return lax.ppermute(value, axis, [(source, source + steps) for source in range(first, last)])


def rotary(values_in, positions):
    half_width = values_in.shape[-1] // 2
    frequency = jnp.exp(
        jnp.arange(half_width, dtype=jnp.float32) * (-2.0 * math.log(THETA) / values_in.shape[-1])
    )
    angles = positions * frequency
    cosine = jnp.cos(angles)
    sine_part = jnp.sin(angles)
    lower_half = values_in[..., :half_width]
    upper_half = values_in[..., half_width:]
    return jnp.concatenate(
        [
            lower_half * cosine - upper_half * sine_part,
            upper_half * cosine + lower_half * sine_part,
        ],
        axis=-1,
    )


def ring_body(hidden_states, qkv_weight, doc_ids):
    tokens = hidden_states[0]
    row_count = tokens.shape[0]
    projected = jnp.dot(
        tokens,
        lax.all_gather(qkv_weight, "fsdp", axis=0, tiled=True),
        preferred_element_type=jnp.float32,
    )
    ctx_count = lax.axis_size("ctx")
    ctx_index = lax.axis_index("ctx")
    row_start = ctx_index * row_count
    local_index = jnp.arange(row_count, dtype=jnp.int32)
    query_pos = row_start + local_index
    positions = query_pos.astype(jnp.float32)
    queries = rotary(
        projected[:, : HEADS * HD].reshape(row_count, HEADS, HD), positions[:, None, None]
    ).astype(jnp.bfloat16)
    keys_here = rotary(projected[:, HEADS * HD : (HEADS + 1) * HD], positions[:, None]).astype(
        jnp.bfloat16
    )
    values_here = projected[:, (HEADS + 1) * HD :].astype(jnp.bfloat16)
    docs_wire = doc_ids[0]
    scale = 1.0 / math.sqrt(HD)

    def attend(state, key_block, value_block, doc_block, key_first):
        running_max, running_sum, running_acc = state
        scores = (
            jnp.einsum("qhd,kd->hqk", queries, key_block, preferred_element_type=jnp.float32)
            * scale
        )
        key_pos = key_first + jnp.arange(key_block.shape[0], dtype=jnp.int32)
        visible = (key_pos[None, :] <= query_pos[:, None]) & (
            doc_block[None, :] == docs_wire[:, None]
        )
        scores = jnp.where(visible[None], scores, -jnp.inf)
        new_max = jnp.maximum(running_max, jnp.max(scores, axis=-1))
        weights = jnp.exp(scores - new_max[..., None])
        factor = jnp.exp(running_max - new_max)
        new_sum = running_sum * factor + jnp.sum(weights, axis=-1)
        update = jnp.einsum(
            "hqk,kd->hqd",
            weights.astype(jnp.bfloat16),
            value_block,
            preferred_element_type=jnp.float32,
        )
        new_acc = running_acc * factor[..., None] + update
        return (new_max, new_sum, new_acc)

    state = (
        jnp.full((HEADS, row_count), -jnp.inf, jnp.float32),
        jnp.zeros((HEADS, row_count), jnp.float32),
        jnp.zeros((HEADS, row_count, HD), jnp.float32),
    )
    state = attend(state, keys_here, values_here, docs_wire, row_start)
    travelling = (keys_here, values_here, docs_wire)
    for rotation in range(1, ctx_count):
        travelling = shifted((travelling[0], travelling[1], travelling[2]), "ctx", 1)
        key_first = (ctx_index - rotation) * row_count
        arrived = travelling

        def take_block(current):
            return attend(current, arrived[0], arrived[1], arrived[2], key_first)

        def keep_block(current):
            return current

        state = lax.cond(rotation <= ctx_index, take_block, keep_block, state)
    context = state[2] / state[1][..., None]
    context = jnp.transpose(context.astype(jnp.bfloat16), (1, 0, 2)).reshape(row_count, HEADS * HD)
    return context[None]


def flip(value, first_mask, second_mask):
    count = lax.axis_size("fsdp")
    pairs = []
    for chip in range(count):
        pairs.append((chip * 2, (chip ^ first_mask) * 2))
        pairs.append((chip * 2 + 1, (chip ^ second_mask) * 2 + 1))
    return lax.ppermute(value, ("fsdp", "ctx"), pairs)


def swap(value):
    return lax.ppermute(value, "ctx", [(0, 1), (1, 0)])


def after(value, *others):
    return lax.optimization_barrier((value,) + others)[0]


def add_blocks(total, parts, masks, mine_ref, other_ref):
    rows = parts[0].shape[0]
    chip = lax.axis_index("fsdp")
    core = lax.axis_index("ctx")
    sums = [None, None] if total is None else [total[0], total[1]]
    for part, (first_mask, second_mask) in zip(parts, masks):
        source = jnp.where(core == 0, chip ^ first_mask, chip ^ second_mask)
        columns = pl.ds(pl.multiple_of(source * rows, rows), rows)
        weights = part[...]
        for side, ref in enumerate((mine_ref, other_ref)):
            term = jnp.dot(ref[:, columns], weights, preferred_element_type=jnp.float32)
            sums[side] = term if sums[side] is None else sums[side] + term
    return sums


def partial_kernel(masks, begun, *refs):
    count = len(masks)
    mine_ref, other_ref = refs[:2]
    parts = refs[2 : 2 + count]
    rest = refs[2 + count :]
    total = None
    if begun:
        total, rest = rest[0], rest[1:]
    (out_ref,) = rest
    sums = add_blocks(total, parts, masks, mine_ref, other_ref)
    out_ref[0] = sums[0]
    out_ref[1] = sums[1]


def final_kernel(masks, *refs):
    count = len(masks)
    mine_ref, other_ref = refs[:2]
    parts = refs[2 : 2 + count]
    total, cos_ref, sin_ref, keep_ref, send_ref = refs[2 + count :]
    sums = add_blocks(total, parts, masks, mine_ref, other_ref)
    turned = lax.axis_index("ctx") == 1

    def turn(block, cosine, sine):
        swapped = jnp.concatenate([block[:, HD // 2 :], block[:, : HD // 2]], axis=1)
        return (block * cosine + swapped * sine).astype(jnp.bfloat16)

    ends = []
    for side in range(2):
        cosine, sine = cos_ref[side], sin_ref[side]
        blocks = [
            turn(sums[side][:, :HD], cosine, sine),
            turn(sums[side][:, HD : 2 * HD], cosine, sine),
            turn(
                sums[side][:, 2 * HD :],
                jnp.where(turned, cosine, 1.0),
                jnp.where(turned, sine, 0.0),
            ),
        ]
        ends.append(blocks)
    for ref, here, there in ((keep_ref, ends[0], ends[1]), (send_ref, ends[1], ends[0])):
        ref[:, :HD] = here[0]
        ref[:, HD : 2 * HD] = here[1]
        ref[:, 2 * HD : 3 * HD] = here[2]
        ref[:, 3 * HD :] = there[2]


def weigh(queries, keys, visible):
    step, width = visible.shape
    heads = queries.shape[0] // step
    scores = lax.dot_general(
        queries, keys, (((1,), (0,)), ((), ())), preferred_element_type=jnp.float32
    )
    scores = jnp.where(visible[None], scores.reshape(heads, step, width), -jnp.inf)
    top = jnp.max(scores, axis=-1, keepdims=True)
    weights = jnp.exp2((scores - top) * (math.log2(math.e) / math.sqrt(HD)))
    return weights.astype(jnp.bfloat16).reshape(heads * step, width)


def visible_keys(column_ref, row_ref, place, first, last):
    same = column_ref[place, :] == row_ref[:, first:last]
    own = lax.broadcasted_iota(jnp.int32, (STEP, STEP), 1)
    query = lax.broadcasted_iota(jnp.int32, (STEP, STEP), 0)
    width = last - first
    if width == STEP:
        return same & (own <= query)
    return jnp.concatenate([same[:, : width - STEP], same[:, width - STEP :] & (own <= query)], axis=1)


def head_columns(ref, place):
    return jnp.concatenate([ref[place, :HD], ref[place, HD : 2 * HD]], axis=0)


def both_ends(ref):
    return jnp.concatenate([ref[:, 3 * HD :], ref[:, 2 * HD : 3 * HD]], axis=0)


def with_ones(values):
    return jnp.concatenate([values, jnp.ones_like(values)], axis=1)


def early_kernel(keep_ref, column_ref, row_ref, probs_ref, keys_ref):
    rows = keep_ref.shape[0]

    @pl.when(lax.axis_index("ctx") == 1)
    def _():
        keys = both_ends(keep_ref).T
        keys_ref[...] = keys
        for step in range(rows // STEP):
            place = slice(step * STEP, (step + 1) * STEP)
            width = rows + (step + 1) * STEP
            probs_ref[step, :, :width] = weigh(
                head_columns(keep_ref, place),
                keys[:, :width],
                visible_keys(column_ref, row_ref, place, 0, width),
            )


def attention_kernel(
    keep_ref, recv_ref, probs_ref, keys_ref, column_ref, row_ref, out_ref, held, sems
):
    core = lax.axis_index("ctx")
    rows = keep_ref.shape[0]

    def write(step, context, order):
        place = slice(step * STEP, (step + 1) * STEP)
        for head, column in enumerate(order):
            held[place, column * HD : (column + 1) * HD] = context[
                head * STEP : (head + 1) * STEP
            ]
        pltpu.make_async_copy(held.at[place], out_ref.at[place], sems.at[step]).start()

    @pl.when(core == 0)
    def _():
        keys, values = recv_ref[:, 2 * HD : 3 * HD].T, with_ones(keep_ref[:, 2 * HD : 3 * HD])
        for step in range(rows // STEP):
            place = slice(step * STEP, (step + 1) * STEP)
            width = (step + 1) * STEP
            probs = weigh(
                jnp.concatenate(
                    [head_columns(keep_ref, place), head_columns(recv_ref, place)], axis=0
                ),
                keys[:, :width],
                visible_keys(column_ref, row_ref, place, rows, rows + width),
            )
            context = jnp.dot(probs, values[:width], preferred_element_type=jnp.float32)
            write(step, (context[:, :HD] / context[:, HD:]).astype(jnp.bfloat16), (0, 1, 2, 3))

    @pl.when(core == 1)
    def _():
        keys, values = keys_ref[...], with_ones(both_ends(recv_ref))
        for step in range(rows // STEP):
            place = slice(step * STEP, (step + 1) * STEP)
            width = rows + (step + 1) * STEP
            probs = weigh(
                head_columns(recv_ref, place),
                keys[:, :width],
                visible_keys(column_ref, row_ref, place, 0, width),
            )
            probs = jnp.concatenate([probs, probs_ref[step, :, :width]], axis=0)
            context = jnp.dot(probs, values[:width], preferred_element_type=jnp.float32)
            write(step, (context[:, :HD] / context[:, HD:]).astype(jnp.bfloat16), (0, 1, 2, 3))

    for step in range(rows // STEP):
        place = slice(step * STEP, (step + 1) * STEP)
        pltpu.make_async_copy(held.at[place], out_ref.at[place], sems.at[step]).wait()


VMEM = pl.BlockSpec(memory_space=pltpu.VMEM)
ANY = pl.BlockSpec(memory_space=pl.ANY)


def stage_kernel(source_ref, docs_ref, docs_other_ref, out_ref, column_ref, row_ref, sem):
    copy = pltpu.make_async_copy(source_ref, out_ref, sem)
    copy.start()
    rows = docs_ref.shape[1]
    docs = docs_ref[...].astype(jnp.float32)
    row_ref[:, :rows] = docs_other_ref[...].astype(jnp.float32)
    row_ref[:, rows:] = docs
    for first in range(0, rows, STEP):
        place = slice(first, first + STEP)
        column_ref[place, :] = jnp.broadcast_to(docs[:, place], (STEP, STEP)).T[:, :1]
    copy.wait()


def stage(value, docs, docs_other):
    tokens = value.shape[0]
    return pl.pallas_call(
        stage_kernel,
        out_shape=(
            jax.ShapeDtypeStruct(value.shape, value.dtype),
            jax.ShapeDtypeStruct((tokens, 1), jnp.float32),
            jax.ShapeDtypeStruct((1, 2 * tokens), jnp.float32),
        ),
        in_specs=[ANY, VMEM, VMEM],
        out_specs=(VMEM, VMEM, VMEM),
        scratch_shapes=[pltpu.SemaphoreType.DMA],
        compiler_params=pltpu.CompilerParams(vmem_limit_bytes=VMEM_LIMIT),
        cost_estimate=pl.CostEstimate(
            flops=0, bytes_accessed=4 * value.size, transcendentals=0
        ),
    )(value, docs, docs_other)


def own_kernel(weight_ref, out_ref, sems):
    core = lax.axis_index("ctx")
    copies = [
        pltpu.make_async_copy(
            weight_ref.at[:, pl.ds(pl.multiple_of(core * 2 * HD, 2 * HD), 2 * HD)],
            out_ref.at[:, pl.ds(0, 2 * HD)],
            sems.at[0],
        ),
        pltpu.make_async_copy(
            weight_ref.at[:, pl.ds(pl.multiple_of((HEADS + 1 - core) * HD, HD), HD)],
            out_ref.at[:, pl.ds(2 * HD, HD)],
            sems.at[1],
        ),
    ]
    for copy in copies:
        copy.start()
    for copy in copies:
        copy.wait()


def own_columns(weight):
    return pl.pallas_call(
        own_kernel,
        out_shape=jax.ShapeDtypeStruct((weight.shape[0], 3 * HD), weight.dtype),
        in_specs=[ANY],
        out_specs=VMEM,
        scratch_shapes=[pltpu.SemaphoreType.DMA((2,))],
        compiler_params=pltpu.CompilerParams(vmem_limit_bytes=VMEM_LIMIT),
    )(weight)


def partial(mine, other, parts, masks, total=None, tables=None):
    rows, width = parts[0].shape
    tokens = mine.shape[0]
    count = len(parts)
    begun = total is not None
    cost = pl.CostEstimate(
        flops=4 * tokens * rows * width * count,
        bytes_accessed=count * rows * (width + 2 * tokens) * 2 + 16 * tokens * width,
        transcendentals=0,
    )
    params = pltpu.CompilerParams(vmem_limit_bytes=VMEM_LIMIT)
    if tables is None:
        return pl.pallas_call(
            functools.partial(partial_kernel, masks, begun),
            out_shape=jax.ShapeDtypeStruct((2, tokens, width), jnp.float32),
            in_specs=[VMEM] * (2 + count + begun),
            out_specs=VMEM,
            compiler_params=params,
            cost_estimate=cost,
        )(mine, other, *parts, *([total] if begun else []))
    out = jax.ShapeDtypeStruct((tokens, 4 * HD), jnp.bfloat16)
    return pl.pallas_call(
        functools.partial(final_kernel, masks),
        out_shape=(out, out),
        in_specs=[VMEM] * (count + 5),
        out_specs=(VMEM, VMEM),
        compiler_params=params,
        cost_estimate=cost,
    )(mine, other, *parts, total, *tables)


def paired_body(hidden_states, qkv_weight, doc_ids):
    mine = hidden_states[0]
    tokens = mine.shape[0]
    core = lax.axis_index("ctx")
    own = own_columns(qkv_weight)

    frequency = jnp.exp(
        jnp.arange(HD // 2, dtype=jnp.float32) * (-2.0 * math.log(THETA) / HD)
    )
    starts = jnp.stack([core, 1 - core])[:, None] * tokens
    positions = (starts + jnp.arange(tokens, dtype=jnp.int32)[None]).astype(jnp.float32)
    angles = positions[..., None] * frequency
    cosine, sine = jnp.cos(angles), jnp.sin(angles)
    cosines = jnp.concatenate([cosine, cosine], axis=-1)
    sines = jnp.concatenate([-sine, sine], axis=-1)
    other, column, row = stage(swap(mine), doc_ids, swap(doc_ids))
    z1 = flip(own, 4, 4)
    z2 = flip(own, 8, 8)
    a0 = flip(own, 1, 2)
    b0 = flip(own, 2, 1)
    z3 = flip(z2, 4, 4)
    c0 = flip(a0, 2, 1)
    a1 = flip(after(z1, b0), 1, 2)
    K1 = partial(mine, other, [own, z1, z2, a0, b0, z3, c0, a1], [(0, 0), (4, 4), (8, 8), (1, 2), (2, 1), (12, 12), (3, 3), (5, 6)])
    b1 = flip(z1, 2, 1)
    c1 = flip(c0, 4, 4)
    c3 = flip(c0, 12, 12)
    (z2_a2, cosines, sines,) = lax.optimization_barrier(
        (z2, cosines, sines)
    )
    a2 = flip(z2_a2, 1, 2)
    K2 = partial(mine, other, [b1, c1, c3, a2], [(6, 5), (7, 7), (15, 15), (9, 10)], K1)
    b2 = flip(z2, 2, 1)
    c2 = flip(a2, 2, 1)
    (z3_a3, K1,) = lax.optimization_barrier(
        (z3, K1)
    )
    a3 = flip(z3_a3, 1, 2)
    K3 = partial(mine, other, [b2, c2, a3], [(10, 9), (11, 11), (13, 14)], K2)
    b3 = flip(z3, 2, 1)
    keep, send = partial(
        mine, other, [b3], [(14, 13)], K3, (cosines, sines)
    )
    recv = swap(send)
    steps = tokens // STEP
    params = pltpu.CompilerParams(vmem_limit_bytes=VMEM_LIMIT)
    probs, keys = pl.pallas_call(
        early_kernel,
        out_shape=(
            jax.ShapeDtypeStruct((steps, 2 * STEP, 2 * tokens), jnp.bfloat16),
            jax.ShapeDtypeStruct((HD, 2 * tokens), jnp.bfloat16),
        ),
        in_specs=[VMEM] * 3,
        out_specs=(VMEM, VMEM),
        compiler_params=params,
        cost_estimate=pl.CostEstimate(
            flops=4 * tokens * tokens * HD,
            bytes_accessed=4 * tokens * tokens,
            transcendentals=2 * tokens * tokens,
        ),
    )(keep, column, row)
    context = pl.pallas_call(
        attention_kernel,
        out_shape=jax.ShapeDtypeStruct((tokens, HEADS * HD), jnp.bfloat16),
        in_specs=[VMEM] * 6,
        out_specs=ANY,
        scratch_shapes=[
            pltpu.VMEM((tokens, HEADS * HD), jnp.bfloat16),
            pltpu.SemaphoreType.DMA((steps,)),
        ],
        compiler_params=params,
        cost_estimate=pl.CostEstimate(
            flops=8 * HEADS * tokens * tokens * HD,
            bytes_accessed=tokens * HD * 32,
            transcendentals=2 * HEADS * tokens * tokens,
        ),
    )(keep, recv, probs, keys, column, row)
    return context[None]


def solution(mesh):
    in_specs = (P("fsdp", "ctx", None), P("fsdp", None), P("fsdp", "ctx"))
    out_specs = P("fsdp", "ctx", None)
    paired = mesh.shape["fsdp"] == 16 and mesh.shape["ctx"] == 2
    body = paired_body if paired else ring_body
    return jax.shard_map(body, mesh=mesh, in_specs=in_specs, out_specs=out_specs, check_vma=False)
```

```python
import functools
import math

import jax
import jax.numpy as jnp
from jax import lax
from jax.experimental import pallas as pl
from jax.experimental.pallas import tpu as pltpu
from jax.sharding import PartitionSpec as P

HEADS = 4
HD = 128


THETA = 1000000.0

STEP = 128

OWN_PARTS = 4

VMEM_LIMIT = 16 * 1024 * 1024


def shifted(value, axis, steps):
    count = lax.axis_size(axis)
    first, last = (max(0, -steps), min(count, count - steps))
    return lax.ppermute(value, axis, [(source, source + steps) for source in range(first, last)])


def rotary(values_in, positions):
    half_width = values_in.shape[-1] // 2
    frequency = jnp.exp(
        jnp.arange(half_width, dtype=jnp.float32) * (-2.0 * math.log(THETA) / values_in.shape[-1])
    )
    angles = positions * frequency
    cosine = jnp.cos(angles)
    sine_part = jnp.sin(angles)
    lower_half = values_in[..., :half_width]
    upper_half = values_in[..., half_width:]
    return jnp.concatenate(
        [
            lower_half * cosine - upper_half * sine_part,
            upper_half * cosine + lower_half * sine_part,
        ],
        axis=-1,
    )


def ring_body(hidden_states, qkv_weight, doc_ids):
    tokens = hidden_states[0]
    row_count = tokens.shape[0]
    projected = jnp.dot(
        tokens,
        lax.all_gather(qkv_weight, "fsdp", axis=0, tiled=True),
        preferred_element_type=jnp.float32,
    )
    ctx_count = lax.axis_size("ctx")
    ctx_index = lax.axis_index("ctx")
    row_start = ctx_index * row_count
    local_index = jnp.arange(row_count, dtype=jnp.int32)
    query_pos = row_start + local_index
    positions = query_pos.astype(jnp.float32)
    queries = rotary(
        projected[:, : HEADS * HD].reshape(row_count, HEADS, HD), positions[:, None, None]
    ).astype(jnp.bfloat16)
    keys_here = rotary(projected[:, HEADS * HD : (HEADS + 1) * HD], positions[:, None]).astype(
        jnp.bfloat16
    )
    values_here = projected[:, (HEADS + 1) * HD :].astype(jnp.bfloat16)
    docs_wire = doc_ids[0]
    scale = 1.0 / math.sqrt(HD)

    def attend(state, key_block, value_block, doc_block, key_first):
        running_max, running_sum, running_acc = state
        scores = (
            jnp.einsum("qhd,kd->hqk", queries, key_block, preferred_element_type=jnp.float32)
            * scale
        )
        key_pos = key_first + jnp.arange(key_block.shape[0], dtype=jnp.int32)
        visible = (key_pos[None, :] <= query_pos[:, None]) & (
            doc_block[None, :] == docs_wire[:, None]
        )
        scores = jnp.where(visible[None], scores, -jnp.inf)
        new_max = jnp.maximum(running_max, jnp.max(scores, axis=-1))
        weights = jnp.exp(scores - new_max[..., None])
        factor = jnp.exp(running_max - new_max)
        new_sum = running_sum * factor + jnp.sum(weights, axis=-1)
        update = jnp.einsum(
            "hqk,kd->hqd",
            weights.astype(jnp.bfloat16),
            value_block,
            preferred_element_type=jnp.float32,
        )
        new_acc = running_acc * factor[..., None] + update
        return (new_max, new_sum, new_acc)

    state = (
        jnp.full((HEADS, row_count), -jnp.inf, jnp.float32),
        jnp.zeros((HEADS, row_count), jnp.float32),
        jnp.zeros((HEADS, row_count, HD), jnp.float32),
    )
    state = attend(state, keys_here, values_here, docs_wire, row_start)
    travelling = (keys_here, values_here, docs_wire)
    for rotation in range(1, ctx_count):
        travelling = shifted((travelling[0], travelling[1], travelling[2]), "ctx", 1)
        key_first = (ctx_index - rotation) * row_count
        arrived = travelling

        def take_block(current):
            return attend(current, arrived[0], arrived[1], arrived[2], key_first)

        def keep_block(current):
            return current

        state = lax.cond(rotation <= ctx_index, take_block, keep_block, state)
    context = state[2] / state[1][..., None]
    context = jnp.transpose(context.astype(jnp.bfloat16), (1, 0, 2)).reshape(row_count, HEADS * HD)
    return context[None]


def flip(value, first_mask, second_mask):
    count = lax.axis_size("fsdp")
    pairs = []
    for chip in range(count):
        pairs.append((chip * 2, (chip ^ first_mask) * 2))
        pairs.append((chip * 2 + 1, (chip ^ second_mask) * 2 + 1))
    return lax.ppermute(value, ("fsdp", "ctx"), pairs)


def swap(value):
    return lax.ppermute(value, "ctx", [(0, 1), (1, 0)])


def after(value, *others):
    return lax.optimization_barrier((value,) + others)[0]


def add_blocks(total, parts, masks, late, mine_ref, other_ref, held, sems):
    rows = mine_ref.shape[1] // lax.axis_size("fsdp")
    chip = lax.axis_index("fsdp")
    core = lax.axis_index("ctx")
    copies = [
        pltpu.make_async_copy(part, held.at[place], sems.at[place])
        for place, part in enumerate(parts[late:])
    ]
    for copy in copies:
        copy.start()
    sums = [None, None] if total is None else [total[0], total[1]]
    for place, (part, blocks) in enumerate(zip(parts, masks)):
        if place >= late:
            copies[place - late].wait()
        for number, (first_mask, second_mask) in enumerate(blocks):
            source = jnp.where(core == 0, chip ^ first_mask, chip ^ second_mask)
            columns = pl.ds(pl.multiple_of(source * rows, rows), rows)
            if place < late:
                weights = part[number * rows : (number + 1) * rows]
            else:
                weights = held[place - late]
            for side, ref in enumerate((mine_ref, other_ref)):
                term = jnp.dot(ref[:, columns], weights, preferred_element_type=jnp.float32)
                sums[side] = term if sums[side] is None else sums[side] + term
    return sums


def partial_kernel(masks, late, begun, *refs):
    count = len(masks)
    mine_ref, other_ref = refs[:2]
    parts = refs[2 : 2 + count]
    rest = refs[2 + count :]
    total = None
    if begun:
        total, rest = rest[0], rest[1:]
    out_ref, held, sems = rest
    sums = add_blocks(total, parts, masks, late, mine_ref, other_ref, held, sems)
    out_ref[0] = sums[0]
    out_ref[1] = sums[1]


def final_kernel(masks, late, *refs):
    count = len(masks)
    mine_ref, other_ref = refs[:2]
    parts = refs[2 : 2 + count]
    total, cos_ref, sin_ref, keep_ref, send_ref, held, sems = refs[2 + count :]
    sums = add_blocks(total, parts, masks, late, mine_ref, other_ref, held, sems)
    turned = lax.axis_index("ctx") == 1

    def turn(block, cosine, sine):
        swapped = jnp.concatenate([block[:, HD // 2 :], block[:, : HD // 2]], axis=1)
        return (block * cosine + swapped * sine).astype(jnp.bfloat16)

    ends = []
    for side in range(2):
        cosine, sine = cos_ref[side], sin_ref[side]
        blocks = [
            turn(sums[side][:, :HD], cosine, sine),
            turn(sums[side][:, HD : 2 * HD], cosine, sine),
            turn(
                sums[side][:, 2 * HD :],
                jnp.where(turned, cosine, 1.0),
                jnp.where(turned, sine, 0.0),
            ),
        ]
        ends.append(blocks)
    for ref, here, there in ((keep_ref, ends[0], ends[1]), (send_ref, ends[1], ends[0])):
        ref[:, :HD] = here[0]
        ref[:, HD : 2 * HD] = here[1]
        ref[:, 2 * HD : 3 * HD] = here[2]
        ref[:, 3 * HD :] = there[2]


def weigh(queries, keys, visible):
    step, width = visible.shape
    heads = queries.shape[0] // step
    scores = lax.dot_general(
        queries, keys, (((1,), (0,)), ((), ())), preferred_element_type=jnp.float32
    )
    scores = jnp.where(visible[None], scores.reshape(heads, step, width), -jnp.inf)
    top = jnp.max(scores, axis=-1, keepdims=True)
    weights = jnp.exp2((scores - top) * (math.log2(math.e) / math.sqrt(HD)))
    return weights.astype(jnp.bfloat16).reshape(heads * step, width)


def visible_keys(column_ref, row_ref, place, first, last):
    same = column_ref[place, :] == row_ref[:, first:last]
    own = lax.broadcasted_iota(jnp.int32, (STEP, STEP), 1)
    query = lax.broadcasted_iota(jnp.int32, (STEP, STEP), 0)
    width = last - first
    if width == STEP:
        return same & (own <= query)
    return jnp.concatenate([same[:, : width - STEP], same[:, width - STEP :] & (own <= query)], axis=1)


def head_columns(ref, place):
    return jnp.concatenate([ref[place, :HD], ref[place, HD : 2 * HD]], axis=0)


def both_ends(ref):
    return jnp.concatenate([ref[:, 3 * HD :], ref[:, 2 * HD : 3 * HD]], axis=0)


def with_ones(values):
    return jnp.concatenate([values, jnp.ones_like(values)], axis=1)


def early_kernel(keep_ref, column_ref, row_ref, probs_ref, keys_ref):
    rows = keep_ref.shape[0]

    @pl.when(lax.axis_index("ctx") == 1)
    def _():
        keys = both_ends(keep_ref).T
        keys_ref[...] = keys
        for step in range(rows // STEP):
            place = slice(step * STEP, (step + 1) * STEP)
            width = rows + (step + 1) * STEP
            probs_ref[step, :, :width] = weigh(
                head_columns(keep_ref, place),
                keys[:, :width],
                visible_keys(column_ref, row_ref, place, 0, width),
            )


def attention_kernel(
    keep_ref, recv_ref, probs_ref, keys_ref, column_ref, row_ref, out_ref, held, sems
):
    core = lax.axis_index("ctx")
    rows = keep_ref.shape[0]

    def write(step, context, order):
        place = slice(step * STEP, (step + 1) * STEP)
        for head, column in enumerate(order):
            held[place, column * HD : (column + 1) * HD] = context[
                head * STEP : (head + 1) * STEP
            ]
        pltpu.make_async_copy(held.at[place], out_ref.at[place], sems.at[step]).start()

    @pl.when(core == 0)
    def _():
        keys, values = recv_ref[:, 2 * HD : 3 * HD].T, with_ones(keep_ref[:, 2 * HD : 3 * HD])
        for step in range(rows // STEP):
            place = slice(step * STEP, (step + 1) * STEP)
            width = (step + 1) * STEP
            probs = weigh(
                jnp.concatenate(
                    [head_columns(keep_ref, place), head_columns(recv_ref, place)], axis=0
                ),
                keys[:, :width],
                visible_keys(column_ref, row_ref, place, rows, rows + width),
            )
            context = jnp.dot(probs, values[:width], preferred_element_type=jnp.float32)
            write(step, (context[:, :HD] / context[:, HD:]).astype(jnp.bfloat16), (0, 1, 2, 3))

    @pl.when(core == 1)
    def _():
        keys, values = keys_ref[...], with_ones(both_ends(recv_ref))
        for step in range(rows // STEP):
            place = slice(step * STEP, (step + 1) * STEP)
            width = rows + (step + 1) * STEP
            probs = weigh(
                head_columns(recv_ref, place),
                keys[:, :width],
                visible_keys(column_ref, row_ref, place, 0, width),
            )
            probs = jnp.concatenate([probs, probs_ref[step, :, :width]], axis=0)
            context = jnp.dot(probs, values[:width], preferred_element_type=jnp.float32)
            write(step, (context[:, :HD] / context[:, HD:]).astype(jnp.bfloat16), (0, 1, 2, 3))

    for step in range(rows // STEP):
        place = slice(step * STEP, (step + 1) * STEP)
        pltpu.make_async_copy(held.at[place], out_ref.at[place], sems.at[step]).wait()


VMEM = pl.BlockSpec(memory_space=pltpu.VMEM)
ANY = pl.BlockSpec(memory_space=pl.ANY)


def stage_kernel(source_ref, docs_ref, docs_other_ref, out_ref, column_ref, row_ref, sem):
    copy = pltpu.make_async_copy(source_ref, out_ref, sem)
    copy.start()
    rows = docs_ref.shape[1]
    docs = docs_ref[...].astype(jnp.float32)
    row_ref[:, :rows] = docs_other_ref[...].astype(jnp.float32)
    row_ref[:, rows:] = docs
    for first in range(0, rows, STEP):
        place = slice(first, first + STEP)
        column_ref[place, :] = jnp.broadcast_to(docs[:, place], (STEP, STEP)).T[:, :1]
    copy.wait()


def stage(value, docs, docs_other):
    tokens = value.shape[0]
    return pl.pallas_call(
        stage_kernel,
        out_shape=(
            jax.ShapeDtypeStruct(value.shape, value.dtype),
            jax.ShapeDtypeStruct((tokens, 1), jnp.float32),
            jax.ShapeDtypeStruct((1, 2 * tokens), jnp.float32),
        ),
        in_specs=[ANY, VMEM, VMEM],
        out_specs=(VMEM, VMEM, VMEM),
        scratch_shapes=[pltpu.SemaphoreType.DMA],
        compiler_params=pltpu.CompilerParams(vmem_limit_bytes=VMEM_LIMIT),
        cost_estimate=pl.CostEstimate(
            flops=0, bytes_accessed=4 * value.size, transcendentals=0
        ),
    )(value, docs, docs_other)


def own_kernel(weight_ref, out_ref, sem):
    core = lax.axis_index("ctx")
    rows = weight_ref.shape[0]
    part = rows // OWN_PARTS
    copies = []
    for first in range(0, rows, part):
        place = pl.ds(first, part)
        for column, source, width in (
            (0, pl.multiple_of(core * 2 * HD, 2 * HD), 2 * HD),
            (2 * HD, pl.multiple_of((HEADS + 1 - core) * HD, HD), HD),
        ):
            copies.append(
                pltpu.make_async_copy(
                    weight_ref.at[place, pl.ds(source, width)],
                    out_ref.at[place, pl.ds(column, width)],
                    sem.at[len(copies)],
                )
            )
    for copy in copies:
        copy.start()
    for copy in copies:
        copy.wait()


def own_columns(weight):
    return pl.pallas_call(
        own_kernel,
        out_shape=jax.ShapeDtypeStruct((weight.shape[0], 3 * HD), weight.dtype),
        in_specs=[pl.BlockSpec(memory_space=pltpu.HBM)],
        out_specs=VMEM,
        scratch_shapes=[pltpu.SemaphoreType.DMA((2 * OWN_PARTS,))],
        compiler_params=pltpu.CompilerParams(vmem_limit_bytes=VMEM_LIMIT),
    )(pltpu.with_memory_space_constraint(weight, pltpu.HBM))


def partial(mine, other, parts, masks, total=None, tables=None, late=None):
    width = parts[0].shape[1]
    tokens = mine.shape[0]
    count = len(parts)
    rows = sum(part.shape[0] for part in parts)
    late = count if late is None else late
    begun = total is not None
    cost = pl.CostEstimate(
        flops=4 * tokens * rows * width,
        bytes_accessed=rows * (width + 2 * tokens) * 2 + 16 * tokens * width,
        transcendentals=0,
    )
    part_specs = [VMEM] * late + [ANY] * (count - late)
    scratch = [
        pltpu.VMEM((max(1, count - late),) + parts[-1].shape, mine.dtype),
        pltpu.SemaphoreType.DMA((max(1, count - late),)),
    ]
    params = pltpu.CompilerParams(vmem_limit_bytes=VMEM_LIMIT)
    if tables is None:
        return pl.pallas_call(
            functools.partial(partial_kernel, masks, late, begun),
            out_shape=jax.ShapeDtypeStruct((2, tokens, width), jnp.float32),
            in_specs=[VMEM] * 2 + part_specs + [VMEM] * begun,
            out_specs=VMEM,
            scratch_shapes=scratch,
            compiler_params=params,
            cost_estimate=cost,
        )(mine, other, *parts, *([total] if begun else []))
    out = jax.ShapeDtypeStruct((tokens, 4 * HD), jnp.bfloat16)
    return pl.pallas_call(
        functools.partial(final_kernel, masks, late),
        out_shape=(out, out),
        in_specs=[VMEM] * 2 + part_specs + [VMEM] * 3,
        out_specs=(VMEM, VMEM),
        scratch_shapes=scratch,
        compiler_params=params,
        cost_estimate=cost,
    )(mine, other, *parts, total, *tables)


def paired_body(hidden_states, qkv_weight, doc_ids):
    mine = hidden_states[0]
    tokens = mine.shape[0]
    core = lax.axis_index("ctx")
    own = own_columns(qkv_weight)

    frequency = jnp.exp(
        jnp.arange(HD // 2, dtype=jnp.float32) * (-2.0 * math.log(THETA) / HD)
    )
    starts = jnp.stack([core, 1 - core])[:, None] * tokens
    positions = (starts + jnp.arange(tokens, dtype=jnp.int32)[None]).astype(jnp.float32)
    angles = positions[..., None] * frequency
    cosine, sine = jnp.cos(angles), jnp.sin(angles)
    cosines = jnp.concatenate([cosine, cosine], axis=-1)
    sines = jnp.concatenate([-sine, sine], axis=-1)
    other, column, row = stage(swap(mine), doc_ids, swap(doc_ids))
    z1 = flip(own, 4, 4)
    a0 = flip(own, 1, 2)
    z2 = flip(own, 8, 8)
    a1 = flip(z1, 1, 2)
    (z2_a2, cosines, sines,) = lax.optimization_barrier(
        (z2, cosines, sines)
    )
    a2 = flip(z2_a2, 1, 2)
    own_a0 = jnp.concatenate([own, a0])
    B0 = flip(own_a0, 2, 1)
    K1 = partial(mine, other, [own, z2, a1, a2, B0, z1, a0], [[(0, 0)], [(8, 8)], [(5, 6)], [(9, 10)], [(2, 1), (3, 3)], [(4, 4)], [(1, 2)]], late=5)
    z3 = flip(z2, 4, 4)
    C1 = flip(B0, 4, 4)
    b2 = flip(z2, 2, 1)
    K2 = partial(mine, other, [z3, C1, b2], [[(12, 12)], [(6, 5), (7, 7)], [(10, 9)]], K1)
    a3 = flip(z3, 1, 2)
    c2 = flip(a2, 2, 1)
    (z3_b3, K1,) = lax.optimization_barrier(
        (z3, K1)
    )
    b3 = flip(z3_b3, 2, 1)
    K3 = partial(mine, other, [a3, c2, b3], [[(13, 14)], [(11, 11)], [(14, 13)]], K2)
    c3 = flip(a3, 2, 1)
    keep, send = partial(
        mine, other, [c3], [[(15, 15)]], K3, (cosines, sines)
    )
    recv = swap(send)
    steps = tokens // STEP
    params = pltpu.CompilerParams(vmem_limit_bytes=VMEM_LIMIT)
    probs, keys = pl.pallas_call(
        early_kernel,
        out_shape=(
            jax.ShapeDtypeStruct((steps, 2 * STEP, 2 * tokens), jnp.bfloat16),
            jax.ShapeDtypeStruct((HD, 2 * tokens), jnp.bfloat16),
        ),
        in_specs=[VMEM] * 3,
        out_specs=(VMEM, VMEM),
        compiler_params=params,
        cost_estimate=pl.CostEstimate(
            flops=4 * tokens * tokens * HD,
            bytes_accessed=4 * tokens * tokens,
            transcendentals=2 * tokens * tokens,
        ),
    )(keep, column, row)
    context = pl.pallas_call(
        attention_kernel,
        out_shape=jax.ShapeDtypeStruct((tokens, HEADS * HD), jnp.bfloat16),
        in_specs=[VMEM] * 6,
        out_specs=ANY,
        scratch_shapes=[
            pltpu.VMEM((tokens, HEADS * HD), jnp.bfloat16),
            pltpu.SemaphoreType.DMA((steps,)),
        ],
        compiler_params=params,
        cost_estimate=pl.CostEstimate(
            flops=8 * HEADS * tokens * tokens * HD,
            bytes_accessed=tokens * HD * 32,
            transcendentals=2 * HEADS * tokens * tokens,
        ),
    )(keep, recv, probs, keys, column, row)
    return context[None]


def solution(mesh):
    in_specs = (P("fsdp", "ctx", None), P("fsdp", None), P("fsdp", "ctx"))
    out_specs = P("fsdp", "ctx", None)
    paired = mesh.shape["fsdp"] == 16 and mesh.shape["ctx"] == 2
    body = paired_body if paired else ring_body
    return jax.shard_map(body, mesh=mesh, in_specs=in_specs, out_specs=out_specs, check_vma=False)
```

```python
import functools
import math

import jax
import jax.numpy as jnp
from jax import lax
from jax.experimental import pallas as pl
from jax.experimental.pallas import tpu as pltpu
from jax.sharding import PartitionSpec as P

HEADS = 4
HD = 128


THETA = 1000000.0

STEP = 128

OWN_PARTS = 4

VMEM_LIMIT = 16 * 1024 * 1024


def shifted(value, axis, steps):
    count = lax.axis_size(axis)
    first, last = (max(0, -steps), min(count, count - steps))
    return lax.ppermute(value, axis, [(source, source + steps) for source in range(first, last)])


def rotary(values_in, positions):
    half_width = values_in.shape[-1] // 2
    frequency = jnp.exp(
        jnp.arange(half_width, dtype=jnp.float32) * (-2.0 * math.log(THETA) / values_in.shape[-1])
    )
    angles = positions * frequency
    cosine = jnp.cos(angles)
    sine_part = jnp.sin(angles)
    lower_half = values_in[..., :half_width]
    upper_half = values_in[..., half_width:]
    return jnp.concatenate(
        [
            lower_half * cosine - upper_half * sine_part,
            upper_half * cosine + lower_half * sine_part,
        ],
        axis=-1,
    )


def ring_body(hidden_states, qkv_weight, doc_ids):
    tokens = hidden_states[0]
    row_count = tokens.shape[0]
    projected = jnp.dot(
        tokens,
        lax.all_gather(qkv_weight, "fsdp", axis=0, tiled=True),
        preferred_element_type=jnp.float32,
    )
    ctx_count = lax.axis_size("ctx")
    ctx_index = lax.axis_index("ctx")
    row_start = ctx_index * row_count
    local_index = jnp.arange(row_count, dtype=jnp.int32)
    query_pos = row_start + local_index
    positions = query_pos.astype(jnp.float32)
    queries = rotary(
        projected[:, : HEADS * HD].reshape(row_count, HEADS, HD), positions[:, None, None]
    ).astype(jnp.bfloat16)
    keys_here = rotary(projected[:, HEADS * HD : (HEADS + 1) * HD], positions[:, None]).astype(
        jnp.bfloat16
    )
    values_here = projected[:, (HEADS + 1) * HD :].astype(jnp.bfloat16)
    docs_wire = doc_ids[0]
    scale = 1.0 / math.sqrt(HD)

    def attend(state, key_block, value_block, doc_block, key_first):
        running_max, running_sum, running_acc = state
        scores = (
            jnp.einsum("qhd,kd->hqk", queries, key_block, preferred_element_type=jnp.float32)
            * scale
        )
        key_pos = key_first + jnp.arange(key_block.shape[0], dtype=jnp.int32)
        visible = (key_pos[None, :] <= query_pos[:, None]) & (
            doc_block[None, :] == docs_wire[:, None]
        )
        scores = jnp.where(visible[None], scores, -jnp.inf)
        new_max = jnp.maximum(running_max, jnp.max(scores, axis=-1))
        weights = jnp.exp(scores - new_max[..., None])
        factor = jnp.exp(running_max - new_max)
        new_sum = running_sum * factor + jnp.sum(weights, axis=-1)
        update = jnp.einsum(
            "hqk,kd->hqd",
            weights.astype(jnp.bfloat16),
            value_block,
            preferred_element_type=jnp.float32,
        )
        new_acc = running_acc * factor[..., None] + update
        return (new_max, new_sum, new_acc)

    state = (
        jnp.full((HEADS, row_count), -jnp.inf, jnp.float32),
        jnp.zeros((HEADS, row_count), jnp.float32),
        jnp.zeros((HEADS, row_count, HD), jnp.float32),
    )
    state = attend(state, keys_here, values_here, docs_wire, row_start)
    travelling = (keys_here, values_here, docs_wire)
    for rotation in range(1, ctx_count):
        travelling = shifted((travelling[0], travelling[1], travelling[2]), "ctx", 1)
        key_first = (ctx_index - rotation) * row_count
        arrived = travelling

        def take_block(current):
            return attend(current, arrived[0], arrived[1], arrived[2], key_first)

        def keep_block(current):
            return current

        state = lax.cond(rotation <= ctx_index, take_block, keep_block, state)
    context = state[2] / state[1][..., None]
    context = jnp.transpose(context.astype(jnp.bfloat16), (1, 0, 2)).reshape(row_count, HEADS * HD)
    return context[None]


def flip(value, first_mask, second_mask):
    count = lax.axis_size("fsdp")
    pairs = []
    for chip in range(count):
        pairs.append((chip * 2, (chip ^ first_mask) * 2))
        pairs.append((chip * 2 + 1, (chip ^ second_mask) * 2 + 1))
    return lax.ppermute(value, ("fsdp", "ctx"), pairs)


def swap(value):
    return lax.ppermute(value, "ctx", [(0, 1), (1, 0)])


def after(value, *others):
    return lax.optimization_barrier((value,) + others)[0]


def add_blocks(total, parts, masks, late, mine_ref, other_ref, held, sems):
    rows = mine_ref.shape[1] // lax.axis_size("fsdp")
    chip = lax.axis_index("fsdp")
    core = lax.axis_index("ctx")
    copies = [
        pltpu.make_async_copy(part, held.at[place], sems.at[place])
        for place, part in enumerate(parts[late:])
    ]
    for copy in copies:
        copy.start()
    sums = [None, None] if total is None else [total[0], total[1]]
    for place, (part, blocks) in enumerate(zip(parts, masks)):
        if place >= late:
            copies[place - late].wait()
        for number, (first_mask, second_mask) in enumerate(blocks):
            source = jnp.where(core == 0, chip ^ first_mask, chip ^ second_mask)
            columns = pl.ds(pl.multiple_of(source * rows, rows), rows)
            if place < late:
                weights = part[number * rows : (number + 1) * rows]
            else:
                weights = held[place - late]
            for side, ref in enumerate((mine_ref, other_ref)):
                term = jnp.dot(ref[:, columns], weights, preferred_element_type=jnp.float32)
                sums[side] = term if sums[side] is None else sums[side] + term
    return sums


def partial_kernel(masks, late, begun, *refs):
    count = len(masks)
    mine_ref, other_ref = refs[:2]
    parts = refs[2 : 2 + count]
    rest = refs[2 + count :]
    total = None
    if begun:
        total, rest = rest[0], rest[1:]
    out_ref, held, sems = rest
    sums = add_blocks(total, parts, masks, late, mine_ref, other_ref, held, sems)
    out_ref[0] = sums[0]
    out_ref[1] = sums[1]


def final_kernel(masks, late, *refs):
    count = len(masks)
    mine_ref, other_ref = refs[:2]
    parts = refs[2 : 2 + count]
    total, cos_ref, sin_ref, keep_ref, send_ref, held, sems = refs[2 + count :]
    sums = add_blocks(total, parts, masks, late, mine_ref, other_ref, held, sems)
    turned = lax.axis_index("ctx") == 1

    def turn(block, cosine, sine):
        swapped = jnp.concatenate([block[:, HD // 2 :], block[:, : HD // 2]], axis=1)
        return (block * cosine + swapped * sine).astype(jnp.bfloat16)

    ends = []
    for side in range(2):
        cosine, sine = cos_ref[side], sin_ref[side]
        blocks = [
            turn(sums[side][:, :HD], cosine, sine),
            turn(sums[side][:, HD : 2 * HD], cosine, sine),
            turn(
                sums[side][:, 2 * HD :],
                jnp.where(turned, cosine, 1.0),
                jnp.where(turned, sine, 0.0),
            ),
        ]
        ends.append(blocks)
    for ref, here, there in ((keep_ref, ends[0], ends[1]), (send_ref, ends[1], ends[0])):
        ref[:, :HD] = here[0]
        ref[:, HD : 2 * HD] = here[1]
        ref[:, 2 * HD : 3 * HD] = here[2]
        ref[:, 3 * HD :] = there[2]


def weigh(queries, keys, visible):
    step, width = visible.shape
    heads = queries.shape[0] // step
    scores = lax.dot_general(
        queries, keys, (((1,), (0,)), ((), ())), preferred_element_type=jnp.float32
    )
    scores = jnp.where(visible[None], scores.reshape(heads, step, width), -jnp.inf)
    top = jnp.max(scores, axis=-1, keepdims=True)
    weights = jnp.exp2((scores - top) * (math.log2(math.e) / math.sqrt(HD)))
    return weights.astype(jnp.bfloat16).reshape(heads * step, width)


def visible_keys(column_ref, row_ref, place, first, last):
    same = column_ref[place, :] == row_ref[:, first:last]
    own = lax.broadcasted_iota(jnp.int32, (STEP, STEP), 1)
    query = lax.broadcasted_iota(jnp.int32, (STEP, STEP), 0)
    width = last - first
    if width == STEP:
        return same & (own <= query)
    return jnp.concatenate([same[:, : width - STEP], same[:, width - STEP :] & (own <= query)], axis=1)


def head_columns(ref, place):
    return jnp.concatenate([ref[place, :HD], ref[place, HD : 2 * HD]], axis=0)


def both_ends(ref):
    return jnp.concatenate([ref[:, 3 * HD :], ref[:, 2 * HD : 3 * HD]], axis=0)


def with_ones(values):
    return jnp.concatenate([values, jnp.ones_like(values)], axis=1)


def early_kernel(keep_ref, column_ref, row_ref, probs_ref, keys_ref):
    rows = keep_ref.shape[0]

    @pl.when(lax.axis_index("ctx") == 1)
    def _():
        keys = both_ends(keep_ref).T
        keys_ref[...] = keys
        for step in range(rows // STEP):
            place = slice(step * STEP, (step + 1) * STEP)
            width = rows + (step + 1) * STEP
            probs_ref[step, :, :width] = weigh(
                head_columns(keep_ref, place),
                keys[:, :width],
                visible_keys(column_ref, row_ref, place, 0, width),
            )


def attention_kernel(
    keep_ref, recv_ref, probs_ref, keys_ref, column_ref, row_ref, out_ref, held, sems
):
    core = lax.axis_index("ctx")
    rows = keep_ref.shape[0]

    def write(step, context, order):
        place = slice(step * STEP, (step + 1) * STEP)
        for head, column in enumerate(order):
            held[place, column * HD : (column + 1) * HD] = context[
                head * STEP : (head + 1) * STEP
            ]
        pltpu.make_async_copy(held.at[place], out_ref.at[place], sems.at[step]).start()

    @pl.when(core == 0)
    def _():
        keys, values = recv_ref[:, 2 * HD : 3 * HD].T, with_ones(keep_ref[:, 2 * HD : 3 * HD])
        for step in range(rows // STEP):
            place = slice(step * STEP, (step + 1) * STEP)
            width = (step + 1) * STEP
            probs = weigh(
                jnp.concatenate(
                    [head_columns(keep_ref, place), head_columns(recv_ref, place)], axis=0
                ),
                keys[:, :width],
                visible_keys(column_ref, row_ref, place, rows, rows + width),
            )
            context = jnp.dot(probs, values[:width], preferred_element_type=jnp.float32)
            write(step, (context[:, :HD] / context[:, HD:]).astype(jnp.bfloat16), (0, 1, 2, 3))

    @pl.when(core == 1)
    def _():
        keys, values = keys_ref[...], with_ones(both_ends(recv_ref))
        for step in range(rows // STEP):
            place = slice(step * STEP, (step + 1) * STEP)
            width = rows + (step + 1) * STEP
            probs = weigh(
                head_columns(recv_ref, place),
                keys[:, :width],
                visible_keys(column_ref, row_ref, place, 0, width),
            )
            probs = jnp.concatenate([probs, probs_ref[step, :, :width]], axis=0)
            context = jnp.dot(probs, values[:width], preferred_element_type=jnp.float32)
            write(step, (context[:, :HD] / context[:, HD:]).astype(jnp.bfloat16), (0, 1, 2, 3))

    for step in range(rows // STEP):
        place = slice(step * STEP, (step + 1) * STEP)
        pltpu.make_async_copy(held.at[place], out_ref.at[place], sems.at[step]).wait()


VMEM = pl.BlockSpec(memory_space=pltpu.VMEM)
ANY = pl.BlockSpec(memory_space=pl.ANY)


def stage_kernel(source_ref, docs_ref, docs_other_ref, out_ref, column_ref, row_ref, sem):
    copy = pltpu.make_async_copy(source_ref, out_ref, sem)
    copy.start()
    rows = docs_ref.shape[1]
    docs = docs_ref[...].astype(jnp.float32)
    row_ref[:, :rows] = docs_other_ref[...].astype(jnp.float32)
    row_ref[:, rows:] = docs
    for first in range(0, rows, STEP):
        place = slice(first, first + STEP)
        column_ref[place, :] = jnp.broadcast_to(docs[:, place], (STEP, STEP)).T[:, :1]
    copy.wait()


def stage(value, docs, docs_other):
    tokens = value.shape[0]
    return pl.pallas_call(
        stage_kernel,
        out_shape=(
            jax.ShapeDtypeStruct(value.shape, value.dtype),
            jax.ShapeDtypeStruct((tokens, 1), jnp.float32),
            jax.ShapeDtypeStruct((1, 2 * tokens), jnp.float32),
        ),
        in_specs=[ANY, VMEM, VMEM],
        out_specs=(VMEM, VMEM, VMEM),
        scratch_shapes=[pltpu.SemaphoreType.DMA],
        compiler_params=pltpu.CompilerParams(vmem_limit_bytes=VMEM_LIMIT),
        cost_estimate=pl.CostEstimate(
            flops=0, bytes_accessed=4 * value.size, transcendentals=0
        ),
    )(value, docs, docs_other)


def own_kernel(weight_ref, out_ref, sem):
    core = lax.axis_index("ctx")
    rows = weight_ref.shape[0]
    part = rows // OWN_PARTS
    copies = []
    for first in range(0, rows, part):
        place = pl.ds(first, part)
        for column, source, width in (
            (0, pl.multiple_of(core * 2 * HD, 2 * HD), 2 * HD),
            (2 * HD, pl.multiple_of((HEADS + 1 - core) * HD, HD), HD),
        ):
            copies.append(
                pltpu.make_async_copy(
                    weight_ref.at[place, pl.ds(source, width)],
                    out_ref.at[place, pl.ds(column, width)],
                    sem.at[len(copies)],
                )
            )
    for copy in copies:
        copy.start()
    for copy in copies:
        copy.wait()


def own_columns(weight):
    return pl.pallas_call(
        own_kernel,
        out_shape=jax.ShapeDtypeStruct((weight.shape[0], 3 * HD), weight.dtype),
        in_specs=[pl.BlockSpec(memory_space=pltpu.HBM)],
        out_specs=VMEM,
        scratch_shapes=[pltpu.SemaphoreType.DMA((2 * OWN_PARTS,))],
        compiler_params=pltpu.CompilerParams(vmem_limit_bytes=VMEM_LIMIT),
    )(pltpu.with_memory_space_constraint(weight, pltpu.HBM))


def partial(mine, other, parts, masks, total=None, tables=None, late=None):
    width = parts[0].shape[1]
    tokens = mine.shape[0]
    count = len(parts)
    rows = sum(part.shape[0] for part in parts)
    late = count if late is None else late
    begun = total is not None
    cost = pl.CostEstimate(
        flops=4 * tokens * rows * width,
        bytes_accessed=rows * (width + 2 * tokens) * 2 + 16 * tokens * width,
        transcendentals=0,
    )
    part_specs = [VMEM] * late + [ANY] * (count - late)
    scratch = [
        pltpu.VMEM((max(1, count - late),) + parts[-1].shape, mine.dtype),
        pltpu.SemaphoreType.DMA((max(1, count - late),)),
    ]
    params = pltpu.CompilerParams(vmem_limit_bytes=VMEM_LIMIT)
    if tables is None:
        return pl.pallas_call(
            functools.partial(partial_kernel, masks, late, begun),
            out_shape=jax.ShapeDtypeStruct((2, tokens, width), jnp.float32),
            in_specs=[VMEM] * 2 + part_specs + [VMEM] * begun,
            out_specs=VMEM,
            scratch_shapes=scratch,
            compiler_params=params,
            cost_estimate=cost,
        )(mine, other, *parts, *([total] if begun else []))
    out = jax.ShapeDtypeStruct((tokens, 4 * HD), jnp.bfloat16)
    return pl.pallas_call(
        functools.partial(final_kernel, masks, late),
        out_shape=(out, out),
        in_specs=[VMEM] * 2 + part_specs + [VMEM] * 3,
        out_specs=(VMEM, VMEM),
        scratch_shapes=scratch,
        compiler_params=params,
        cost_estimate=cost,
    )(mine, other, *parts, total, *tables)


def paired_body(hidden_states, qkv_weight, doc_ids):
    mine = hidden_states[0]
    tokens = mine.shape[0]
    core = lax.axis_index("ctx")
    own = own_columns(qkv_weight)

    frequency = jnp.exp(
        jnp.arange(HD // 2, dtype=jnp.float32) * (-2.0 * math.log(THETA) / HD)
    )
    starts = jnp.stack([core, 1 - core])[:, None] * tokens
    positions = (starts + jnp.arange(tokens, dtype=jnp.int32)[None]).astype(jnp.float32)
    angles = positions[..., None] * frequency
    cosine, sine = jnp.cos(angles), jnp.sin(angles)
    cosines = jnp.concatenate([cosine, cosine], axis=-1)
    sines = jnp.concatenate([-sine, sine], axis=-1)
    other, column, row = stage(swap(mine), doc_ids, swap(doc_ids))
    z1 = flip(own, 4, 4)
    z2 = flip(own, 8, 8)
    (z2_a2, cosines, sines,) = lax.optimization_barrier(
        (z2, cosines, sines)
    )
    a2 = flip(z2_a2, 1, 2)
    z3 = flip(z2, 4, 4)
    a1 = flip(z1, 1, 2)
    a0 = flip(own, 1, 2)
    K1 = partial(mine, other, [own, z2, a2, z3, a1, z1, a0], [[(0, 0)], [(8, 8)], [(9, 10)], [(12, 12)], [(5, 6)], [(4, 4)], [(1, 2)]], late=5)
    own_a0 = jnp.concatenate([own, a0])
    B0 = flip(own_a0, 2, 1)
    b2 = flip(z2, 2, 1)
    a3 = flip(z3, 1, 2)
    K2 = partial(mine, other, [B0, b2, a3], [[(2, 1), (3, 3)], [(10, 9)], [(13, 14)]], K1)
    C1 = flip(B0, 4, 4)
    c2 = flip(a2, 2, 1)
    (z3_b3, K1,) = lax.optimization_barrier(
        (z3, K1)
    )
    b3 = flip(z3_b3, 2, 1)
    K3 = partial(mine, other, [C1, c2, b3], [[(6, 5), (7, 7)], [(11, 11)], [(14, 13)]], K2)
    c3 = flip(a3, 2, 1)
    keep, send = partial(
        mine, other, [c3], [[(15, 15)]], K3, (cosines, sines)
    )
    recv = swap(send)
    steps = tokens // STEP
    params = pltpu.CompilerParams(vmem_limit_bytes=VMEM_LIMIT)
    probs, keys = pl.pallas_call(
        early_kernel,
        out_shape=(
            jax.ShapeDtypeStruct((steps, 2 * STEP, 2 * tokens), jnp.bfloat16),
            jax.ShapeDtypeStruct((HD, 2 * tokens), jnp.bfloat16),
        ),
        in_specs=[VMEM] * 3,
        out_specs=(VMEM, VMEM),
        compiler_params=params,
        cost_estimate=pl.CostEstimate(
            flops=4 * tokens * tokens * HD,
            bytes_accessed=4 * tokens * tokens,
            transcendentals=2 * tokens * tokens,
        ),
    )(keep, column, row)
    context = pl.pallas_call(
        attention_kernel,
        out_shape=jax.ShapeDtypeStruct((tokens, HEADS * HD), jnp.bfloat16),
        in_specs=[VMEM] * 6,
        out_specs=ANY,
        scratch_shapes=[
            pltpu.VMEM((tokens, HEADS * HD), jnp.bfloat16),
            pltpu.SemaphoreType.DMA((steps,)),
        ],
        compiler_params=params,
        cost_estimate=pl.CostEstimate(
            flops=8 * HEADS * tokens * tokens * HD,
            bytes_accessed=tokens * HD * 32,
            transcendentals=2 * HEADS * tokens * tokens,
        ),
    )(keep, recv, probs, keys, column, row)
    return context[None]


def solution(mesh):
    in_specs = (P("fsdp", "ctx", None), P("fsdp", None), P("fsdp", "ctx"))
    out_specs = P("fsdp", "ctx", None)
    paired = mesh.shape["fsdp"] == 16 and mesh.shape["ctx"] == 2
    body = paired_body if paired else ring_body
    return jax.shard_map(body, mesh=mesh, in_specs=in_specs, out_specs=out_specs, check_vma=False)
```

```python
import functools
import math

import jax
import jax.numpy as jnp
from jax import lax
from jax.experimental import pallas as pl
from jax.experimental.pallas import tpu as pltpu
from jax.sharding import PartitionSpec as P

HEADS = 4
HD = 128


THETA = 1000000.0

STEP = 128

OWN_PARTS = 4

VMEM_LIMIT = 16 * 1024 * 1024


def shifted(value, axis, steps):
    count = lax.axis_size(axis)
    first, last = (max(0, -steps), min(count, count - steps))
    return lax.ppermute(value, axis, [(source, source + steps) for source in range(first, last)])


def rotary(values_in, positions):
    half_width = values_in.shape[-1] // 2
    frequency = jnp.exp(
        jnp.arange(half_width, dtype=jnp.float32) * (-2.0 * math.log(THETA) / values_in.shape[-1])
    )
    angles = positions * frequency
    cosine = jnp.cos(angles)
    sine_part = jnp.sin(angles)
    lower_half = values_in[..., :half_width]
    upper_half = values_in[..., half_width:]
    return jnp.concatenate(
        [
            lower_half * cosine - upper_half * sine_part,
            upper_half * cosine + lower_half * sine_part,
        ],
        axis=-1,
    )


def ring_body(hidden_states, qkv_weight, doc_ids):
    tokens = hidden_states[0]
    row_count = tokens.shape[0]
    projected = jnp.dot(
        tokens,
        lax.all_gather(qkv_weight, "fsdp", axis=0, tiled=True),
        preferred_element_type=jnp.float32,
    )
    ctx_count = lax.axis_size("ctx")
    ctx_index = lax.axis_index("ctx")
    row_start = ctx_index * row_count
    local_index = jnp.arange(row_count, dtype=jnp.int32)
    query_pos = row_start + local_index
    positions = query_pos.astype(jnp.float32)
    queries = rotary(
        projected[:, : HEADS * HD].reshape(row_count, HEADS, HD), positions[:, None, None]
    ).astype(jnp.bfloat16)
    keys_here = rotary(projected[:, HEADS * HD : (HEADS + 1) * HD], positions[:, None]).astype(
        jnp.bfloat16
    )
    values_here = projected[:, (HEADS + 1) * HD :].astype(jnp.bfloat16)
    docs_wire = doc_ids[0]
    scale = 1.0 / math.sqrt(HD)

    def attend(state, key_block, value_block, doc_block, key_first):
        running_max, running_sum, running_acc = state
        scores = (
            jnp.einsum("qhd,kd->hqk", queries, key_block, preferred_element_type=jnp.float32)
            * scale
        )
        key_pos = key_first + jnp.arange(key_block.shape[0], dtype=jnp.int32)
        visible = (key_pos[None, :] <= query_pos[:, None]) & (
            doc_block[None, :] == docs_wire[:, None]
        )
        scores = jnp.where(visible[None], scores, -jnp.inf)
        new_max = jnp.maximum(running_max, jnp.max(scores, axis=-1))
        weights = jnp.exp(scores - new_max[..., None])
        factor = jnp.exp(running_max - new_max)
        new_sum = running_sum * factor + jnp.sum(weights, axis=-1)
        update = jnp.einsum(
            "hqk,kd->hqd",
            weights.astype(jnp.bfloat16),
            value_block,
            preferred_element_type=jnp.float32,
        )
        new_acc = running_acc * factor[..., None] + update
        return (new_max, new_sum, new_acc)

    state = (
        jnp.full((HEADS, row_count), -jnp.inf, jnp.float32),
        jnp.zeros((HEADS, row_count), jnp.float32),
        jnp.zeros((HEADS, row_count, HD), jnp.float32),
    )
    state = attend(state, keys_here, values_here, docs_wire, row_start)
    travelling = (keys_here, values_here, docs_wire)
    for rotation in range(1, ctx_count):
        travelling = shifted((travelling[0], travelling[1], travelling[2]), "ctx", 1)
        key_first = (ctx_index - rotation) * row_count
        arrived = travelling

        def take_block(current):
            return attend(current, arrived[0], arrived[1], arrived[2], key_first)

        def keep_block(current):
            return current

        state = lax.cond(rotation <= ctx_index, take_block, keep_block, state)
    context = state[2] / state[1][..., None]
    context = jnp.transpose(context.astype(jnp.bfloat16), (1, 0, 2)).reshape(row_count, HEADS * HD)
    return context[None]


def flip(value, first_mask, second_mask):
    count = lax.axis_size("fsdp")
    pairs = []
    for chip in range(count):
        pairs.append((chip * 2, (chip ^ first_mask) * 2))
        pairs.append((chip * 2 + 1, (chip ^ second_mask) * 2 + 1))
    return lax.ppermute(value, ("fsdp", "ctx"), pairs)


def swap(value):
    return lax.ppermute(value, "ctx", [(0, 1), (1, 0)])


def after(value, *others):
    return lax.optimization_barrier((value,) + others)[0]


def add_blocks(total, parts, masks, late, mine_ref, other_ref, held, sems):
    rows = mine_ref.shape[1] // lax.axis_size("fsdp")
    chip = lax.axis_index("fsdp")
    core = lax.axis_index("ctx")
    copies = [
        pltpu.make_async_copy(part, held.at[place], sems.at[place])
        for place, part in enumerate(parts[late:])
    ]
    for copy in copies:
        copy.start()
    sums = [None, None] if total is None else [total[0], total[1]]
    for place, (part, blocks) in enumerate(zip(parts, masks)):
        if place >= late:
            copies[place - late].wait()
        for number, (first_mask, second_mask) in enumerate(blocks):
            source = jnp.where(core == 0, chip ^ first_mask, chip ^ second_mask)
            columns = pl.ds(pl.multiple_of(source * rows, rows), rows)
            if place < late:
                weights = part[number * rows : (number + 1) * rows]
            else:
                weights = held[place - late]
            for side, ref in enumerate((mine_ref, other_ref)):
                term = jnp.dot(ref[:, columns], weights, preferred_element_type=jnp.float32)
                sums[side] = term if sums[side] is None else sums[side] + term
    return sums


def partial_kernel(masks, late, begun, *refs):
    count = len(masks)
    mine_ref, other_ref = refs[:2]
    parts = refs[2 : 2 + count]
    rest = refs[2 + count :]
    total = None
    if begun:
        total, rest = rest[0], rest[1:]
    out_ref, held, sems = rest
    sums = add_blocks(total, parts, masks, late, mine_ref, other_ref, held, sems)
    out_ref[0] = sums[0]
    out_ref[1] = sums[1]


def final_kernel(masks, late, *refs):
    count = len(masks)
    mine_ref, other_ref = refs[:2]
    parts = refs[2 : 2 + count]
    total, cos_ref, sin_ref, keep_ref, send_ref, held, sems = refs[2 + count :]
    sums = add_blocks(total, parts, masks, late, mine_ref, other_ref, held, sems)
    turned = lax.axis_index("ctx") == 1

    def turn(block, cosine, sine):
        swapped = jnp.concatenate([block[:, HD // 2 :], block[:, : HD // 2]], axis=1)
        return (block * cosine + swapped * sine).astype(jnp.bfloat16)

    ends = []
    for side in range(2):
        cosine, sine = cos_ref[side], sin_ref[side]
        blocks = [
            turn(sums[side][:, :HD], cosine, sine),
            turn(sums[side][:, HD : 2 * HD], cosine, sine),
            turn(
                sums[side][:, 2 * HD :],
                jnp.where(turned, cosine, 1.0),
                jnp.where(turned, sine, 0.0),
            ),
        ]
        ends.append(blocks)
    for ref, here, there in ((keep_ref, ends[0], ends[1]), (send_ref, ends[1], ends[0])):
        ref[:, :HD] = here[0]
        ref[:, HD : 2 * HD] = here[1]
        ref[:, 2 * HD : 3 * HD] = here[2]
        ref[:, 3 * HD :] = there[2]


def weigh(queries, keys, visible):
    step, width = visible.shape
    heads = queries.shape[0] // step
    scores = lax.dot_general(
        queries, keys, (((1,), (0,)), ((), ())), preferred_element_type=jnp.float32
    )
    scores = jnp.where(visible[None], scores.reshape(heads, step, width), -jnp.inf)
    top = jnp.max(scores, axis=-1, keepdims=True)
    weights = jnp.exp2((scores - top) * (math.log2(math.e) / math.sqrt(HD)))
    return weights.astype(jnp.bfloat16).reshape(heads * step, width)


def visible_keys(column_ref, row_ref, place, first, last):
    same = column_ref[place, :] == row_ref[:, first:last]
    own = lax.broadcasted_iota(jnp.int32, (STEP, STEP), 1)
    query = lax.broadcasted_iota(jnp.int32, (STEP, STEP), 0)
    width = last - first
    if width == STEP:
        return same & (own <= query)
    return jnp.concatenate([same[:, : width - STEP], same[:, width - STEP :] & (own <= query)], axis=1)


def head_columns(ref, place):
    return jnp.concatenate([ref[place, :HD], ref[place, HD : 2 * HD]], axis=0)


def both_ends(ref):
    return jnp.concatenate([ref[:, 3 * HD :], ref[:, 2 * HD : 3 * HD]], axis=0)


def with_ones(values):
    return jnp.concatenate([values, jnp.ones_like(values)], axis=1)


def early_kernel(keep_ref, column_ref, row_ref, probs_ref, keys_ref):
    rows = keep_ref.shape[0]

    @pl.when(lax.axis_index("ctx") == 1)
    def _():
        keys = both_ends(keep_ref).T
        keys_ref[...] = keys
        for step in range(rows // STEP):
            place = slice(step * STEP, (step + 1) * STEP)
            width = rows + (step + 1) * STEP
            probs_ref[step, :, :width] = weigh(
                head_columns(keep_ref, place),
                keys[:, :width],
                visible_keys(column_ref, row_ref, place, 0, width),
            )


def attention_kernel(
    keep_ref, recv_ref, probs_ref, keys_ref, column_ref, row_ref, out_ref, held, sems
):
    core = lax.axis_index("ctx")
    rows = keep_ref.shape[0]

    def write(step, context, order):
        place = slice(step * STEP, (step + 1) * STEP)
        for head, column in enumerate(order):
            held[place, column * HD : (column + 1) * HD] = context[
                head * STEP : (head + 1) * STEP
            ]
        pltpu.make_async_copy(held.at[place], out_ref.at[place], sems.at[step]).start()

    @pl.when(core == 0)
    def _():
        keys, values = recv_ref[:, 2 * HD : 3 * HD].T, with_ones(keep_ref[:, 2 * HD : 3 * HD])
        for step in range(rows // STEP):
            place = slice(step * STEP, (step + 1) * STEP)
            width = (step + 1) * STEP
            probs = weigh(
                jnp.concatenate(
                    [head_columns(keep_ref, place), head_columns(recv_ref, place)], axis=0
                ),
                keys[:, :width],
                visible_keys(column_ref, row_ref, place, rows, rows + width),
            )
            context = jnp.dot(probs, values[:width], preferred_element_type=jnp.float32)
            write(step, (context[:, :HD] / context[:, HD:]).astype(jnp.bfloat16), (0, 1, 2, 3))

    @pl.when(core == 1)
    def _():
        keys, values = keys_ref[...], with_ones(both_ends(recv_ref))
        for step in range(rows // STEP):
            place = slice(step * STEP, (step + 1) * STEP)
            width = rows + (step + 1) * STEP
            probs = weigh(
                head_columns(recv_ref, place),
                keys[:, :width],
                visible_keys(column_ref, row_ref, place, 0, width),
            )
            context = jnp.concatenate(
                [
                    jnp.dot(part, values[:width], preferred_element_type=jnp.float32)
                    for part in (probs, probs_ref[step, :, :width])
                ],
                axis=0,
            )
            write(step, (context[:, :HD] / context[:, HD:]).astype(jnp.bfloat16), (0, 1, 2, 3))

    for step in range(rows // STEP):
        place = slice(step * STEP, (step + 1) * STEP)
        pltpu.make_async_copy(held.at[place], out_ref.at[place], sems.at[step]).wait()


VMEM = pl.BlockSpec(memory_space=pltpu.VMEM)
ANY = pl.BlockSpec(memory_space=pl.ANY)


def stage_kernel(source_ref, docs_ref, docs_other_ref, out_ref, column_ref, row_ref, sem):
    copy = pltpu.make_async_copy(source_ref, out_ref, sem)
    copy.start()
    rows = docs_ref.shape[1]
    docs = docs_ref[...].astype(jnp.float32)
    row_ref[:, :rows] = docs_other_ref[...].astype(jnp.float32)
    row_ref[:, rows:] = docs
    for first in range(0, rows, STEP):
        place = slice(first, first + STEP)
        column_ref[place, :] = jnp.broadcast_to(docs[:, place], (STEP, STEP)).T[:, :1]
    copy.wait()


def stage(value, docs, docs_other):
    tokens = value.shape[0]
    return pl.pallas_call(
        stage_kernel,
        out_shape=(
            jax.ShapeDtypeStruct(value.shape, value.dtype),
            jax.ShapeDtypeStruct((tokens, 1), jnp.float32),
            jax.ShapeDtypeStruct((1, 2 * tokens), jnp.float32),
        ),
        in_specs=[ANY, VMEM, VMEM],
        out_specs=(VMEM, VMEM, VMEM),
        scratch_shapes=[pltpu.SemaphoreType.DMA],
        compiler_params=pltpu.CompilerParams(vmem_limit_bytes=VMEM_LIMIT),
        cost_estimate=pl.CostEstimate(
            flops=0, bytes_accessed=4 * value.size, transcendentals=0
        ),
    )(value, docs, docs_other)


def own_kernel(weight_ref, out_ref, sem):
    core = lax.axis_index("ctx")
    rows = weight_ref.shape[0]
    part = rows // OWN_PARTS
    copies = []
    for first in range(0, rows, part):
        place = pl.ds(first, part)
        for column, source, width in (
            (0, pl.multiple_of(core * 2 * HD, 2 * HD), 2 * HD),
            (2 * HD, pl.multiple_of((HEADS + 1 - core) * HD, HD), HD),
        ):
            copies.append(
                pltpu.make_async_copy(
                    weight_ref.at[place, pl.ds(source, width)],
                    out_ref.at[place, pl.ds(column, width)],
                    sem.at[len(copies)],
                )
            )
    for copy in copies:
        copy.start()
    for copy in copies:
        copy.wait()


def own_columns(weight):
    return pl.pallas_call(
        own_kernel,
        out_shape=jax.ShapeDtypeStruct((weight.shape[0], 3 * HD), weight.dtype),
        in_specs=[pl.BlockSpec(memory_space=pltpu.HBM)],
        out_specs=VMEM,
        scratch_shapes=[pltpu.SemaphoreType.DMA((2 * OWN_PARTS,))],
        compiler_params=pltpu.CompilerParams(vmem_limit_bytes=VMEM_LIMIT),
    )(pltpu.with_memory_space_constraint(weight, pltpu.HBM))


def partial(mine, other, parts, masks, total=None, tables=None, late=None):
    width = parts[0].shape[1]
    tokens = mine.shape[0]
    count = len(parts)
    rows = sum(part.shape[0] for part in parts)
    late = count if late is None else late
    begun = total is not None
    cost = pl.CostEstimate(
        flops=4 * tokens * rows * width,
        bytes_accessed=rows * (width + 2 * tokens) * 2 + 16 * tokens * width,
        transcendentals=0,
    )
    part_specs = [VMEM] * late + [ANY] * (count - late)
    scratch = [
        pltpu.VMEM((max(1, count - late),) + parts[-1].shape, mine.dtype),
        pltpu.SemaphoreType.DMA((max(1, count - late),)),
    ]
    params = pltpu.CompilerParams(vmem_limit_bytes=VMEM_LIMIT)
    if tables is None:
        return pl.pallas_call(
            functools.partial(partial_kernel, masks, late, begun),
            out_shape=jax.ShapeDtypeStruct((2, tokens, width), jnp.float32),
            in_specs=[VMEM] * 2 + part_specs + [VMEM] * begun,
            out_specs=VMEM,
            scratch_shapes=scratch,
            compiler_params=params,
            cost_estimate=cost,
        )(mine, other, *parts, *([total] if begun else []))
    out = jax.ShapeDtypeStruct((tokens, 4 * HD), jnp.bfloat16)
    return pl.pallas_call(
        functools.partial(final_kernel, masks, late),
        out_shape=(out, out),
        in_specs=[VMEM] * 2 + part_specs + [VMEM] * 3,
        out_specs=(VMEM, VMEM),
        scratch_shapes=scratch,
        compiler_params=params,
        cost_estimate=cost,
    )(mine, other, *parts, total, *tables)


def paired_body(hidden_states, qkv_weight, doc_ids):
    mine = hidden_states[0]
    tokens = mine.shape[0]
    core = lax.axis_index("ctx")
    own = own_columns(qkv_weight)

    frequency = jnp.exp(
        jnp.arange(HD // 2, dtype=jnp.float32) * (-2.0 * math.log(THETA) / HD)
    )
    starts = jnp.stack([core, 1 - core])[:, None] * tokens
    positions = (starts + jnp.arange(tokens, dtype=jnp.int32)[None]).astype(jnp.float32)
    angles = positions[..., None] * frequency
    cosine, sine = jnp.cos(angles), jnp.sin(angles)
    cosines = jnp.concatenate([cosine, cosine], axis=-1)
    sines = jnp.concatenate([-sine, sine], axis=-1)
    other, column, row = stage(swap(after(mine, own)), doc_ids, swap(after(doc_ids, own)))
    z1 = flip(own, 4, 4)
    z2 = flip(own, 8, 8)
    (z2_a2, cosines, sines,) = lax.optimization_barrier(
        (z2, cosines, sines)
    )
    a2 = flip(z2_a2, 1, 2)
    z3 = flip(z2, 4, 4)
    a1 = flip(z1, 1, 2)
    a0 = flip(own, 1, 2)
    K1 = partial(mine, other, [own, z2, a2, z3, a1, z1, a0], [[(0, 0)], [(8, 8)], [(9, 10)], [(12, 12)], [(5, 6)], [(4, 4)], [(1, 2)]], late=5)
    own_a0 = jnp.concatenate([own, a0])
    B0 = flip(own_a0, 2, 1)
    C1 = flip(B0, 4, 4)
    a3 = flip(z3, 1, 2)
    K2 = partial(mine, other, [B0, C1, a3], [[(2, 1), (3, 3)], [(6, 5), (7, 7)], [(13, 14)]], K1)
    b2 = flip(z2, 2, 1)
    c2 = flip(a2, 2, 1)
    (z3_b3, K1,) = lax.optimization_barrier(
        (z3, K1)
    )
    b3 = flip(z3_b3, 2, 1)
    K3 = partial(mine, other, [b2, c2, b3], [[(10, 9)], [(11, 11)], [(14, 13)]], K2)
    c3 = flip(a3, 2, 1)
    keep, send = partial(
        mine, other, [c3], [[(15, 15)]], K3, (cosines, sines)
    )
    recv = swap(send)
    steps = tokens // STEP
    params = pltpu.CompilerParams(vmem_limit_bytes=VMEM_LIMIT)
    probs, keys = pl.pallas_call(
        early_kernel,
        out_shape=(
            jax.ShapeDtypeStruct((steps, 2 * STEP, 2 * tokens), jnp.bfloat16),
            jax.ShapeDtypeStruct((HD, 2 * tokens), jnp.bfloat16),
        ),
        in_specs=[VMEM] * 3,
        out_specs=(VMEM, VMEM),
        compiler_params=params,
        cost_estimate=pl.CostEstimate(
            flops=4 * tokens * tokens * HD,
            bytes_accessed=4 * tokens * tokens,
            transcendentals=2 * tokens * tokens,
        ),
    )(keep, column, row)
    context = pl.pallas_call(
        attention_kernel,
        out_shape=jax.ShapeDtypeStruct((tokens, HEADS * HD), jnp.bfloat16),
        in_specs=[VMEM] * 6,
        out_specs=ANY,
        scratch_shapes=[
            pltpu.VMEM((tokens, HEADS * HD), jnp.bfloat16),
            pltpu.SemaphoreType.DMA((steps,)),
        ],
        compiler_params=params,
        cost_estimate=pl.CostEstimate(
            flops=8 * HEADS * tokens * tokens * HD,
            bytes_accessed=tokens * HD * 32,
            transcendentals=2 * HEADS * tokens * tokens,
        ),
    )(keep, recv, probs, keys, column, row)
    return context[None]


def solution(mesh):
    in_specs = (P("fsdp", "ctx", None), P("fsdp", None), P("fsdp", "ctx"))
    out_specs = P("fsdp", "ctx", None)
    paired = mesh.shape["fsdp"] == 16 and mesh.shape["ctx"] == 2
    body = paired_body if paired else ring_body
    return jax.shard_map(body, mesh=mesh, in_specs=in_specs, out_specs=out_specs, check_vma=False)
```

```python
import functools
import math

import jax
import jax.numpy as jnp
from jax import lax
from jax.experimental import pallas as pl
from jax.experimental.pallas import tpu as pltpu
from jax.sharding import PartitionSpec as P

HEADS = 4
HD = 128


THETA = 1000000.0

STEP = 128

OWN_PARTS = 1

VMEM_LIMIT = 16 * 1024 * 1024


def shifted(value, axis, steps):
    count = lax.axis_size(axis)
    first, last = (max(0, -steps), min(count, count - steps))
    return lax.ppermute(value, axis, [(source, source + steps) for source in range(first, last)])


def rotary(values_in, positions):
    half_width = values_in.shape[-1] // 2
    frequency = jnp.exp(
        jnp.arange(half_width, dtype=jnp.float32) * (-2.0 * math.log(THETA) / values_in.shape[-1])
    )
    angles = positions * frequency
    cosine = jnp.cos(angles)
    sine_part = jnp.sin(angles)
    lower_half = values_in[..., :half_width]
    upper_half = values_in[..., half_width:]
    return jnp.concatenate(
        [
            lower_half * cosine - upper_half * sine_part,
            upper_half * cosine + lower_half * sine_part,
        ],
        axis=-1,
    )


def ring_body(hidden_states, qkv_weight, doc_ids):
    tokens = hidden_states[0]
    row_count = tokens.shape[0]
    projected = jnp.dot(
        tokens,
        lax.all_gather(qkv_weight, "fsdp", axis=0, tiled=True),
        preferred_element_type=jnp.float32,
    )
    ctx_count = lax.axis_size("ctx")
    ctx_index = lax.axis_index("ctx")
    row_start = ctx_index * row_count
    local_index = jnp.arange(row_count, dtype=jnp.int32)
    query_pos = row_start + local_index
    positions = query_pos.astype(jnp.float32)
    queries = rotary(
        projected[:, : HEADS * HD].reshape(row_count, HEADS, HD), positions[:, None, None]
    ).astype(jnp.bfloat16)
    keys_here = rotary(projected[:, HEADS * HD : (HEADS + 1) * HD], positions[:, None]).astype(
        jnp.bfloat16
    )
    values_here = projected[:, (HEADS + 1) * HD :].astype(jnp.bfloat16)
    docs_wire = doc_ids[0]
    scale = 1.0 / math.sqrt(HD)

    def attend(state, key_block, value_block, doc_block, key_first):
        running_max, running_sum, running_acc = state
        scores = (
            jnp.einsum("qhd,kd->hqk", queries, key_block, preferred_element_type=jnp.float32)
            * scale
        )
        key_pos = key_first + jnp.arange(key_block.shape[0], dtype=jnp.int32)
        visible = (key_pos[None, :] <= query_pos[:, None]) & (
            doc_block[None, :] == docs_wire[:, None]
        )
        scores = jnp.where(visible[None], scores, -jnp.inf)
        new_max = jnp.maximum(running_max, jnp.max(scores, axis=-1))
        weights = jnp.exp(scores - new_max[..., None])
        factor = jnp.exp(running_max - new_max)
        new_sum = running_sum * factor + jnp.sum(weights, axis=-1)
        update = jnp.einsum(
            "hqk,kd->hqd",
            weights.astype(jnp.bfloat16),
            value_block,
            preferred_element_type=jnp.float32,
        )
        new_acc = running_acc * factor[..., None] + update
        return (new_max, new_sum, new_acc)

    state = (
        jnp.full((HEADS, row_count), -jnp.inf, jnp.float32),
        jnp.zeros((HEADS, row_count), jnp.float32),
        jnp.zeros((HEADS, row_count, HD), jnp.float32),
    )
    state = attend(state, keys_here, values_here, docs_wire, row_start)
    travelling = (keys_here, values_here, docs_wire)
    for rotation in range(1, ctx_count):
        travelling = shifted((travelling[0], travelling[1], travelling[2]), "ctx", 1)
        key_first = (ctx_index - rotation) * row_count
        arrived = travelling

        def take_block(current):
            return attend(current, arrived[0], arrived[1], arrived[2], key_first)

        def keep_block(current):
            return current

        state = lax.cond(rotation <= ctx_index, take_block, keep_block, state)
    context = state[2] / state[1][..., None]
    context = jnp.transpose(context.astype(jnp.bfloat16), (1, 0, 2)).reshape(row_count, HEADS * HD)
    return context[None]


def flip(value, first_mask, second_mask):
    count = lax.axis_size("fsdp")
    pairs = []
    for chip in range(count):
        pairs.append((chip * 2, (chip ^ first_mask) * 2))
        pairs.append((chip * 2 + 1, (chip ^ second_mask) * 2 + 1))
    return lax.ppermute(value, ("fsdp", "ctx"), pairs)


def swap(value):
    return lax.ppermute(value, "ctx", [(0, 1), (1, 0)])


def after(value, *others):
    return lax.optimization_barrier((value,) + others)[0]


def add_blocks(total, parts, masks, late, mine_ref, other_ref, held, sems):
    rows = mine_ref.shape[1] // lax.axis_size("fsdp")
    chip = lax.axis_index("fsdp")
    core = lax.axis_index("ctx")
    copies = [
        pltpu.make_async_copy(part, held.at[place], sems.at[place])
        for place, part in enumerate(parts[late:])
    ]
    for copy in copies:
        copy.start()
    sums = [None, None] if total is None else [total[0], total[1]]
    for place, (part, blocks) in enumerate(zip(parts, masks)):
        if place >= late:
            copies[place - late].wait()
        for number, (first_mask, second_mask) in enumerate(blocks):
            source = jnp.where(core == 0, chip ^ first_mask, chip ^ second_mask)
            columns = pl.ds(pl.multiple_of(source * rows, rows), rows)
            if place < late:
                weights = part[number * rows : (number + 1) * rows]
            else:
                weights = held[place - late]
            for side, ref in enumerate((mine_ref, other_ref)):
                term = jnp.dot(ref[:, columns], weights, preferred_element_type=jnp.float32)
                sums[side] = term if sums[side] is None else sums[side] + term
    return sums


def partial_kernel(masks, late, begun, *refs):
    count = len(masks)
    mine_ref, other_ref = refs[:2]
    parts = refs[2 : 2 + count]
    rest = refs[2 + count :]
    total = None
    if begun:
        total, rest = rest[0], rest[1:]
    out_ref, held, sems = rest
    sums = add_blocks(total, parts, masks, late, mine_ref, other_ref, held, sems)
    out_ref[0] = sums[0]
    out_ref[1] = sums[1]


def final_kernel(masks, late, *refs):
    count = len(masks)
    mine_ref, other_ref = refs[:2]
    parts = refs[2 : 2 + count]
    total, cos_ref, sin_ref, keep_ref, send_ref, held, sems = refs[2 + count :]
    sums = add_blocks(total, parts, masks, late, mine_ref, other_ref, held, sems)
    turned = lax.axis_index("ctx") == 1

    def turn(block, cosine, sine):
        swapped = jnp.concatenate([block[:, HD // 2 :], block[:, : HD // 2]], axis=1)
        return (block * cosine + swapped * sine).astype(jnp.bfloat16)

    ends = []
    for side in range(2):
        cosine, sine = cos_ref[side], sin_ref[side]
        blocks = [
            turn(sums[side][:, :HD], cosine, sine),
            turn(sums[side][:, HD : 2 * HD], cosine, sine),
            turn(
                sums[side][:, 2 * HD :],
                jnp.where(turned, cosine, 1.0),
                jnp.where(turned, sine, 0.0),
            ),
        ]
        ends.append(blocks)
    for ref, here, there in ((keep_ref, ends[0], ends[1]), (send_ref, ends[1], ends[0])):
        ref[:, :HD] = here[0]
        ref[:, HD : 2 * HD] = here[1]
        ref[:, 2 * HD : 3 * HD] = here[2]
        ref[:, 3 * HD :] = there[2]


def weigh(queries, keys, visible):
    step, width = visible.shape
    heads = queries.shape[0] // step
    scores = lax.dot_general(
        queries, keys, (((1,), (0,)), ((), ())), preferred_element_type=jnp.float32
    )
    scores = jnp.where(visible[None], scores.reshape(heads, step, width), -jnp.inf)
    top = jnp.max(scores, axis=-1, keepdims=True)
    weights = jnp.exp2((scores - top) * (math.log2(math.e) / math.sqrt(HD)))
    return weights.astype(jnp.bfloat16).reshape(heads * step, width)


def visible_keys(column_ref, row_ref, place, first, last):
    same = column_ref[place, :] == row_ref[:, first:last]
    own = lax.broadcasted_iota(jnp.int32, (STEP, STEP), 1)
    query = lax.broadcasted_iota(jnp.int32, (STEP, STEP), 0)
    width = last - first
    if width == STEP:
        return same & (own <= query)
    return jnp.concatenate([same[:, : width - STEP], same[:, width - STEP :] & (own <= query)], axis=1)


def head_columns(ref, place):
    return jnp.concatenate([ref[place, :HD], ref[place, HD : 2 * HD]], axis=0)


def both_ends(ref):
    return jnp.concatenate([ref[:, 3 * HD :], ref[:, 2 * HD : 3 * HD]], axis=0)


def with_ones(values):
    return jnp.concatenate([values, jnp.ones_like(values)], axis=1)


def early_kernel(keep_ref, column_ref, row_ref, probs_ref, keys_ref):
    rows = keep_ref.shape[0]

    @pl.when(lax.axis_index("ctx") == 1)
    def _():
        keys = both_ends(keep_ref).T
        keys_ref[...] = keys
        for step in range(rows // STEP):
            place = slice(step * STEP, (step + 1) * STEP)
            width = rows + (step + 1) * STEP
            probs_ref[step, :, :width] = weigh(
                head_columns(keep_ref, place),
                keys[:, :width],
                visible_keys(column_ref, row_ref, place, 0, width),
            )


def attention_kernel(
    keep_ref, recv_ref, probs_ref, keys_ref, column_ref, row_ref, out_ref, held, sems
):
    core = lax.axis_index("ctx")
    rows = keep_ref.shape[0]

    def write(step, context, order):
        place = slice(step * STEP, (step + 1) * STEP)
        for head, column in enumerate(order):
            held[place, column * HD : (column + 1) * HD] = context[
                head * STEP : (head + 1) * STEP
            ]
        pltpu.make_async_copy(held.at[place], out_ref.at[place], sems.at[step]).start()

    @pl.when(core == 0)
    def _():
        keys, values = recv_ref[:, 2 * HD : 3 * HD].T, with_ones(keep_ref[:, 2 * HD : 3 * HD])
        for step in range(rows // STEP):
            place = slice(step * STEP, (step + 1) * STEP)
            width = (step + 1) * STEP
            probs = weigh(
                jnp.concatenate(
                    [head_columns(keep_ref, place), head_columns(recv_ref, place)], axis=0
                ),
                keys[:, :width],
                visible_keys(column_ref, row_ref, place, rows, rows + width),
            )
            context = jnp.dot(probs, values[:width], preferred_element_type=jnp.float32)
            write(step, (context[:, :HD] / context[:, HD:]).astype(jnp.bfloat16), (0, 1, 2, 3))

    @pl.when(core == 1)
    def _():
        keys, values = keys_ref[...], with_ones(both_ends(recv_ref))
        for step in range(rows // STEP):
            place = slice(step * STEP, (step + 1) * STEP)
            width = rows + (step + 1) * STEP
            probs = weigh(
                head_columns(recv_ref, place),
                keys[:, :width],
                visible_keys(column_ref, row_ref, place, 0, width),
            )
            probs = jnp.concatenate([probs, probs_ref[step, :, :width]], axis=0)
            context = jnp.dot(probs, values[:width], preferred_element_type=jnp.float32)
            write(step, (context[:, :HD] / context[:, HD:]).astype(jnp.bfloat16), (0, 1, 2, 3))

    for step in range(rows // STEP):
        place = slice(step * STEP, (step + 1) * STEP)
        pltpu.make_async_copy(held.at[place], out_ref.at[place], sems.at[step]).wait()


VMEM = pl.BlockSpec(memory_space=pltpu.VMEM)
ANY = pl.BlockSpec(memory_space=pl.ANY)


def stage_kernel(source_ref, docs_ref, docs_other_ref, out_ref, column_ref, row_ref, sem):
    copy = pltpu.make_async_copy(source_ref, out_ref, sem)
    copy.start()
    rows = docs_ref.shape[1]
    docs = docs_ref[...].astype(jnp.float32)
    row_ref[:, :rows] = docs_other_ref[...].astype(jnp.float32)
    row_ref[:, rows:] = docs
    for first in range(0, rows, STEP):
        place = slice(first, first + STEP)
        column_ref[place, :] = jnp.broadcast_to(docs[:, place], (STEP, STEP)).T[:, :1]
    copy.wait()


def stage(value, docs, docs_other):
    tokens = value.shape[0]
    return pl.pallas_call(
        stage_kernel,
        out_shape=(
            jax.ShapeDtypeStruct(value.shape, value.dtype),
            jax.ShapeDtypeStruct((tokens, 1), jnp.float32),
            jax.ShapeDtypeStruct((1, 2 * tokens), jnp.float32),
        ),
        in_specs=[ANY, VMEM, VMEM],
        out_specs=(VMEM, VMEM, VMEM),
        scratch_shapes=[pltpu.SemaphoreType.DMA],
        compiler_params=pltpu.CompilerParams(vmem_limit_bytes=VMEM_LIMIT),
        cost_estimate=pl.CostEstimate(
            flops=0, bytes_accessed=4 * value.size, transcendentals=0
        ),
    )(value, docs, docs_other)


def own_kernel(weight_ref, out_ref, sem):
    core = lax.axis_index("ctx")
    rows = weight_ref.shape[0]
    part = rows // OWN_PARTS
    copies = []
    for first in range(0, rows, part):
        place = pl.ds(first, part)
        for column, source, width in (
            (0, pl.multiple_of(core * 2 * HD, 2 * HD), 2 * HD),
            (2 * HD, pl.multiple_of((HEADS + 1 - core) * HD, HD), HD),
        ):
            copies.append(
                pltpu.make_async_copy(
                    weight_ref.at[place, pl.ds(source, width)],
                    out_ref.at[place, pl.ds(column, width)],
                    sem.at[len(copies)],
                )
            )
    for copy in copies:
        copy.start()
    for copy in copies:
        copy.wait()


def own_columns(weight):
    return pl.pallas_call(
        own_kernel,
        out_shape=jax.ShapeDtypeStruct((weight.shape[0], 3 * HD), weight.dtype),
        in_specs=[pl.BlockSpec(memory_space=pltpu.HBM)],
        out_specs=VMEM,
        scratch_shapes=[pltpu.SemaphoreType.DMA((2 * OWN_PARTS,))],
        compiler_params=pltpu.CompilerParams(vmem_limit_bytes=VMEM_LIMIT),
    )(pltpu.with_memory_space_constraint(weight, pltpu.HBM))


def partial(mine, other, parts, masks, total=None, tables=None, late=None):
    width = parts[0].shape[1]
    tokens = mine.shape[0]
    count = len(parts)
    rows = sum(part.shape[0] for part in parts)
    late = count if late is None else late
    begun = total is not None
    cost = pl.CostEstimate(
        flops=4 * tokens * rows * width,
        bytes_accessed=rows * (width + 2 * tokens) * 2 + 16 * tokens * width,
        transcendentals=0,
    )
    part_specs = [VMEM] * late + [ANY] * (count - late)
    scratch = [
        pltpu.VMEM((max(1, count - late),) + parts[-1].shape, mine.dtype),
        pltpu.SemaphoreType.DMA((max(1, count - late),)),
    ]
    params = pltpu.CompilerParams(vmem_limit_bytes=VMEM_LIMIT)
    if tables is None:
        return pl.pallas_call(
            functools.partial(partial_kernel, masks, late, begun),
            out_shape=jax.ShapeDtypeStruct((2, tokens, width), jnp.float32),
            in_specs=[VMEM] * 2 + part_specs + [VMEM] * begun,
            out_specs=VMEM,
            scratch_shapes=scratch,
            compiler_params=params,
            cost_estimate=cost,
        )(mine, other, *parts, *([total] if begun else []))
    out = jax.ShapeDtypeStruct((tokens, 4 * HD), jnp.bfloat16)
    return pl.pallas_call(
        functools.partial(final_kernel, masks, late),
        out_shape=(out, out),
        in_specs=[VMEM] * 2 + part_specs + [VMEM] * 3,
        out_specs=(VMEM, VMEM),
        scratch_shapes=scratch,
        compiler_params=params,
        cost_estimate=cost,
    )(mine, other, *parts, total, *tables)


def paired_body(hidden_states, qkv_weight, doc_ids):
    mine = hidden_states[0]
    tokens = mine.shape[0]
    core = lax.axis_index("ctx")
    own = own_columns(qkv_weight)

    frequency = jnp.exp(
        jnp.arange(HD // 2, dtype=jnp.float32) * (-2.0 * math.log(THETA) / HD)
    )
    starts = jnp.stack([core, 1 - core])[:, None] * tokens
    positions = (starts + jnp.arange(tokens, dtype=jnp.int32)[None]).astype(jnp.float32)
    angles = positions[..., None] * frequency
    cosine, sine = jnp.cos(angles), jnp.sin(angles)
    cosines = jnp.concatenate([cosine, cosine], axis=-1)
    sines = jnp.concatenate([-sine, sine], axis=-1)
    other, column, row = stage(swap(mine), doc_ids, swap(doc_ids))
    z1 = flip(own, 4, 4)
    z2 = flip(own, 8, 8)
    (z2_a2, cosines, sines,) = lax.optimization_barrier(
        (z2, cosines, sines)
    )
    a2 = flip(z2_a2, 1, 2)
    z3 = flip(z2, 4, 4)
    a1 = flip(z1, 1, 2)
    a0 = flip(own, 1, 2)
    K1 = partial(mine, other, [own, z2, a2, z3, a1, z1, a0], [[(0, 0)], [(8, 8)], [(9, 10)], [(12, 12)], [(5, 6)], [(4, 4)], [(1, 2)]], late=5)
    own_a0 = jnp.concatenate([own, a0])
    B0 = flip(own_a0, 2, 1)
    b2 = flip(z2, 2, 1)
    a3 = flip(z3, 1, 2)
    K2 = partial(mine, other, [B0, b2, a3], [[(2, 1), (3, 3)], [(10, 9)], [(13, 14)]], K1)
    C1 = flip(B0, 4, 4)
    c2 = flip(a2, 2, 1)
    (z3_b3, K1,) = lax.optimization_barrier(
        (z3, K1)
    )
    b3 = flip(z3_b3, 2, 1)
    K3 = partial(mine, other, [C1, c2, b3], [[(6, 5), (7, 7)], [(11, 11)], [(14, 13)]], K2)
    c3 = flip(a3, 2, 1)
    keep, send = partial(
        mine, other, [c3], [[(15, 15)]], K3, (cosines, sines)
    )
    recv = swap(send)
    steps = tokens // STEP
    params = pltpu.CompilerParams(vmem_limit_bytes=VMEM_LIMIT)
    probs, keys = pl.pallas_call(
        early_kernel,
        out_shape=(
            jax.ShapeDtypeStruct((steps, 2 * STEP, 2 * tokens), jnp.bfloat16),
            jax.ShapeDtypeStruct((HD, 2 * tokens), jnp.bfloat16),
        ),
        in_specs=[VMEM] * 3,
        out_specs=(VMEM, VMEM),
        compiler_params=params,
        cost_estimate=pl.CostEstimate(
            flops=4 * tokens * tokens * HD,
            bytes_accessed=4 * tokens * tokens,
            transcendentals=2 * tokens * tokens,
        ),
    )(keep, column, row)
    context = pl.pallas_call(
        attention_kernel,
        out_shape=jax.ShapeDtypeStruct((tokens, HEADS * HD), jnp.bfloat16),
        in_specs=[VMEM] * 6,
        out_specs=ANY,
        scratch_shapes=[
            pltpu.VMEM((tokens, HEADS * HD), jnp.bfloat16),
            pltpu.SemaphoreType.DMA((steps,)),
        ],
        compiler_params=params,
        cost_estimate=pl.CostEstimate(
            flops=8 * HEADS * tokens * tokens * HD,
            bytes_accessed=tokens * HD * 32,
            transcendentals=2 * HEADS * tokens * tokens,
        ),
    )(keep, recv, probs, keys, column, row)
    return context[None]


def solution(mesh):
    in_specs = (P("fsdp", "ctx", None), P("fsdp", None), P("fsdp", "ctx"))
    out_specs = P("fsdp", "ctx", None)
    paired = mesh.shape["fsdp"] == 16 and mesh.shape["ctx"] == 2
    body = paired_body if paired else ring_body
    return jax.shard_map(body, mesh=mesh, in_specs=in_specs, out_specs=out_specs, check_vma=False)
```
